32 devices in a mesh: grp: 2 (over y), row: 4 (over z), col: 4 (over x, core).
Axes of the slice: x: 2, y: 2, z: 4, core: 2. Of those that a mesh axis runs over, the one named last changes fastest.
Arguments:
- activations: bfloat16 [1024, 6144], P(('grp', 'col'), 'row'), parts along dimension 0, may hold values from -6 to 6
- out_grads: bfloat16 [1024, 18432], P(('grp', 'row'), 'col'), parts along dimension 0, may hold values from -0.1796875 to 0.1796875
- matrix: bfloat16 [12288, 18432], P(('grp', 'row'), 'col'), parts along dimension 0, may hold values from -30 to 30
- left: bfloat16 [12288, 256], P(('grp', 'row')), parts along dimension 0, may hold values from -4 to 4
- right: bfloat16 [36864, 256], P(('grp', 'col')), parts along dimension 0, may hold values from -4 to 4
Outputs:
- left_new: bfloat16 [12288, 256], P(('grp', 'row')), parts along dimension 0
- right_new: bfloat16 [36864, 256], P(('grp', 'col')), parts along dimension 0
- residual: bfloat16 [12288, 18432], P(('grp', 'row'), 'col'), parts along dimension 0
The draws below stay inside these ranges and needn't reach their ends.
There are 2 independent parts, one for each index of `grp`. The reference program is written for one: setup_inputs(seed, part) draws one part's arguments, and reference() takes and returns one part's arrays. A program takes and returns all parts, laid end to end along the dimension named above; each array names one. Nothing has to cross between parts.
All inputs are finite; a program needn't handle non-finite values.
Results may differ from the reference program's by a relative error of at most 0.0034.
Values may be sent and summed in bfloat16 or wider, within the bound.
No kernel may reach another device: no remote copies, remote signals or barrier semaphores. Data moves between devices by JAX's collectives and lax.ppermute only.
A program may use at most 192 MiB of HBM per device.

```python
import math
import jax
import jax.numpy as jnp
from jax import lax

M = 6144
N = 18432
RANK = 256
TOKENS = 512


def factor_base(key, shape):
    return jnp.clip(jax.random.normal(key, shape, jnp.float32), -6.0, 6.0)


def factor_parts(key):
    keys = jax.random.split(jax.random.fold_in(key, 53), 6)
    row_scale = jnp.exp(jax.random.uniform(keys[0], (M, 1), jnp.float32, 0.0, math.log(10.0)))
    column_pos = jnp.arange(N, dtype=jnp.float32)[:, None] / N
    col_scale = jnp.exp(column_pos * math.log(3.0) + jax.random.uniform(keys[1], (N, 1), jnp.float32, -0.5, 0.5))
    left_spread = 0.8 / math.sqrt(RANK)
    right_spread = 0.1
    left_full = jnp.clip(row_scale * left_spread * factor_base(keys[2], (M, RANK)), -4.0, 4.0)
    left_target = left_full + row_scale * left_spread * factor_base(keys[3], (M, RANK))
    right_full = jnp.clip(col_scale * right_spread * factor_base(keys[4], (N, RANK)), -4.0, 4.0)
    right_target = right_full + col_scale * right_spread * factor_base(keys[5], (N, RANK))
    return (left_full, right_full, left_target, right_target, row_scale, col_scale)


def draw_left(key, part):
    return factor_parts(key)[0].astype(jnp.bfloat16)


def draw_right(key, part):
    return factor_parts(key)[1].astype(jnp.bfloat16)


def draw_matrix(key, part):
    left_full, right_full, left_target, right_target, row_scale, col_scale = factor_parts(key)
    low_part = jnp.dot(left_target, right_target.T)
    noise_key = jax.random.fold_in(key, 97)
    noise_base = jnp.clip(jax.random.normal(noise_key, (M, N), jnp.float32), -6.0, 6.0)
    noise = 0.03 * noise_base * row_scale * col_scale.T
    return jnp.clip(low_part + noise, -30.0, 30.0).astype(jnp.bfloat16)


def block_scale(stream_key, extent, shards, least, largest):
    def one(axis_at, parts):
        heights = jax.random.uniform(jax.random.fold_in(jax.random.fold_in(stream_key, 6), axis_at), (parts,), jnp.float32, least / len(shards), largest / len(shards))
        return jnp.repeat(jnp.exp(heights), extent[axis_at] // parts).reshape((-1,) + (1,) * (len(extent) - axis_at - 1))

    level = one(*shards[0])
    for cut in shards[1:]:
        level = level * one(*cut)
    return level


def normal_values(rng, dims, deviation, limit, cuts=(), held_as=jnp.bfloat16):
    drawn = jax.random.normal(rng, dims, jnp.float32) * deviation
    if len(cuts) > 0:
        drawn = block_scale(rng, dims, cuts, -0.22, 0.18) * drawn
    return jnp.clip(drawn, min=-limit, max=limit).astype(held_as)


def setup_inputs(seed: int = 0, part: int = 0) -> dict:
    streams_of = jax.random.split(jax.random.key(seed), 6)
    part_splits = jax.random.split(jax.random.fold_in(streams_of[5], part), 6)
    return {
        "activations": normal_values(part_splits[0], (TOKENS, M), 1.0, 6.0, ((0, 4), (1, 4))),
        "out_grads": normal_values(part_splits[1], (TOKENS, N), 0.03, 0.1796875, ((0, 4), (1, 4))),
        "matrix": draw_matrix(jax.random.fold_in(jax.random.fold_in(streams_of[5], part), 71), part),
        "left": draw_left(jax.random.fold_in(jax.random.fold_in(streams_of[5], part), 71), part),
        "right": draw_right(jax.random.fold_in(jax.random.fold_in(streams_of[5], part), 71), part),
    }


epsilon = 1e-6


def contract_rank(first, second):
    return lax.dot_general(first, second, (((1,), (1,)), ((), ())), preferred_element_type=jnp.float32)


def reference(activations, out_grads, matrix, left, right):
    gradient = lax.dot_general(activations, out_grads, (((0,), (0,)), ((), ())), preferred_element_type=jnp.float32)
    wfloat = matrix.astype(jnp.float32)
    fisher = 1.0 + (wfloat * gradient) ** 2
    early_residual = wfloat - contract_rank(left, right)
    weighted_early = (fisher * early_residual).astype(jnp.bfloat16)
    left_descent = jnp.dot(weighted_early, right, preferred_element_type=jnp.float32)
    left_image = contract_rank(left_descent.astype(jnp.bfloat16), right)
    left_step = jnp.sum(left_descent * left_descent) / (jnp.sum(fisher * left_image * left_image) + epsilon)
    left_new = (left.astype(jnp.float32) + left_step * left_descent).astype(jnp.bfloat16)
    later_residual = early_residual - left_step * left_image
    weighted_later = (fisher * later_residual).astype(jnp.bfloat16)
    right_descent = lax.dot_general(weighted_later, left_new, (((0,), (0,)), ((), ())), preferred_element_type=jnp.float32)
    right_image = contract_rank(left_new, right_descent.astype(jnp.bfloat16))
    right_step = jnp.sum(right_descent * right_descent) / (jnp.sum(fisher * right_image * right_image) + epsilon)
    right_new = (right.astype(jnp.float32) + right_step * right_descent).astype(jnp.bfloat16)
    residual = (later_residual - right_step * right_image).astype(jnp.bfloat16)
    return left_new, right_new, residual
```

```python
import functools
import jax
import jax.numpy as jnp
from jax import lax
from jax.experimental import pallas as pl
from jax.experimental.pallas import tpu as pltpu
from jax.sharding import PartitionSpec as P

f32 = jnp.float32
bf16 = jnp.bfloat16
NT = (((1,), (1,)), ((), ()))
BLOCK = 768
TILE = 768
MB = 1 << 20


def pick(extent, want, offset=0):
    for size in range(min(want, extent), 0, -1):
        if extent % size == 0 and offset % size == 0 and (size % 128 == 0 or size == extent):
            return size
    return extent


def each(count, unroll, step):
    if unroll:
        for i in range(count):
            step(i)
    else:
        pl.loop(0, count)(step)


def span(i, tile):
    return pl.ds(i * tile, tile) if isinstance(i, int) else pl.ds(pl.multiple_of(i * tile, tile), tile)


UNROLL = True


def fold(x):
    rows, cols = x.shape
    y = x.reshape(rows // 8, 8, cols).sum(axis=0)
    out = y[:, :128]
    for at in range(128, cols, 128):
        out = out + y[:, at:at + 128]
    return out


def first_kernel(groups, tile, has_prev, *refs):
    at_ref, w_ref, l_ref, r_ref = refs[:4]
    used = 4
    parts = []
    for count in groups:
        parts.append(refs[used:used + count])
        used += count
    if has_prev:
        acc_in = refs[used]
        used += 2
    f_ref, acc_ref, g_ref = refs[used:used + 3]
    step = pl.program_id(0)
    at = 0
    for part in parts:
        total = part[0][...]
        for more in part[1:]:
            total = total + more[...]
        g_ref[pl.ds(at, total.shape[0]), :] = total
        at += total.shape[0]

    @pl.when(step == 0)
    def _():
        if has_prev:
            acc_ref[...] = acc_in[...]
        else:
            acc_ref[...] = jnp.zeros_like(acc_ref)

    m = at_ref.shape[0]

    def step_rows(i):
        rows = span(i, tile)
        grad = jnp.dot(at_ref[rows, :], g_ref[...], preferred_element_type=f32)
        image = lax.dot_general(l_ref[rows, :], r_ref[...], NT, preferred_element_type=f32)
        w = w_ref[rows, :].astype(f32)
        x = w * grad
        fisher = 1.0 + x * x
        f_ref[rows, :] = fisher.astype(f_ref.dtype)
        weighted = (fisher * (w - image)).astype(bf16)
        acc_ref[rows, :] += jnp.dot(weighted, r_ref[...], preferred_element_type=f32)
    each(m // tile, UNROLL, step_rows)


def first_pass(at, w, left, right, groups, offset, width, prev, block=512, tile=512, fdt=bf16):
    m, n = w.shape
    rank = left.shape[1]
    tokens = at.shape[1]
    bn = pick(width, block, offset)
    tile = pick(m, tile)
    base = offset // bn
    flat = [p for g in groups for p in g]
    ins = [at, w, left, right] + flat
    specs = [
        pl.BlockSpec((m, tokens), lambda j: (0, 0)),
        pl.BlockSpec((m, bn), lambda j: (0, base + j)),
        pl.BlockSpec((m, rank), lambda j: (0, 0)),
        pl.BlockSpec((bn, rank), lambda j: (base + j, 0)),
    ] + [pl.BlockSpec((p.shape[0], bn), lambda j: (0, j)) for p in flat]
    alias = {}
    if prev is not None:
        fprev, accprev = prev
        alias = {len(ins): 1, len(ins) + 1: 0}
        ins += [accprev, fprev]
        specs += [pl.BlockSpec((m, rank), lambda j: (0, 0)), pl.BlockSpec(memory_space=pl.ANY)]
    cost = pl.CostEstimate(flops=2 * m * width * (tokens + 2 * rank), bytes_accessed=m * width * 4, transcendentals=0)
    return pl.pallas_call(
        functools.partial(first_kernel, tuple(len(g) for g in groups), tile, prev is not None),
        grid=(width // bn,),
        in_specs=specs,
        out_specs=[pl.BlockSpec((m, bn), lambda j: (0, base + j)), pl.BlockSpec((m, rank), lambda j: (0, 0))],
        out_shape=[jax.ShapeDtypeStruct((m, n), fdt), jax.ShapeDtypeStruct((m, rank), f32)],
        scratch_shapes=[pltpu.VMEM((tokens, bn), bf16)],
        input_output_aliases=alias,
        compiler_params=pltpu.CompilerParams(vmem_limit_bytes=48 * MB),
        cost_estimate=cost,
        name="first_pass",
    )(*ins)


def curve_kernel(trans, tile, a_ref, b_ref, f_ref, o_ref):
    @pl.when(pl.program_id(0) == 0)
    def _():
        o_ref[...] = jnp.zeros_like(o_ref)
    m = a_ref.shape[0]

    def step_rows(i):
        rows = span(i, tile)
        if trans:
            image = lax.dot_general(a_ref[rows, :], b_ref[...], NT, preferred_element_type=f32)
        else:
            image = jnp.dot(a_ref[rows, :], b_ref[...], preferred_element_type=f32)
        o_ref[...] += fold(f_ref[rows, :].astype(f32) * (image * image))
    each(m // tile, UNROLL, step_rows)


def curve_pass(a, b, f, offset, width, trans, block=512, tile=512):
    m, rank = a.shape
    bn = pick(width, block, offset)
    base = offset // bn
    tile = pick(m, tile)
    bspec = pl.BlockSpec((bn, rank), lambda j: (base + j, 0)) if trans else pl.BlockSpec((rank, bn), lambda j: (0, j))
    return pl.pallas_call(
        functools.partial(curve_kernel, trans, tile),
        grid=(width // bn,),
        in_specs=[pl.BlockSpec((m, rank), lambda j: (0, 0)), bspec, pl.BlockSpec((m, bn), lambda j: (0, base + j))],
        out_specs=pl.BlockSpec((8, 128), lambda j: (0, 0)),
        out_shape=jax.ShapeDtypeStruct((8, 128), f32),
        compiler_params=pltpu.CompilerParams(vmem_limit_bytes=48 * MB),
        cost_estimate=pl.CostEstimate(flops=2 * m * width * rank, bytes_accessed=2 * m * width, transcendentals=0),
        name="curve_pass",
    )(a, b, f)


def partial_kernel(tile, s_ref, w_ref, l_ref, d_ref, r_ref, f_ref, t_ref, o_ref, acc_ref):
    s = s_ref[0, 0]
    m = l_ref.shape[0]
    acc_ref[...] = jnp.zeros_like(acc_ref)

    def step_rows(i):
        rows = span(i, tile)
        early = lax.dot_general(l_ref[rows, :], r_ref[...], NT, preferred_element_type=f32)
        image = lax.dot_general(d_ref[rows, :], r_ref[...], NT, preferred_element_type=f32)
        later = (w_ref[rows, :].astype(f32) - early) - s * image
        weighted = (f_ref[rows, :].astype(f32) * later).astype(bf16)
        acc_ref[...] += jnp.dot(t_ref[:, rows], weighted, preferred_element_type=f32)
    each(m // tile, UNROLL, step_rows)
    o_ref[...] = acc_ref[...].astype(o_ref.dtype)


def partial_pass(s, w, left, descent, right, f, new_t, offset, width, block=512, tile=512):
    m, rank = left.shape
    bn = pick(width, block, offset)
    base = offset // bn
    tile = pick(m, tile)
    whole = pl.BlockSpec((m, rank), lambda j: (0, 0))
    wide = pl.BlockSpec((m, bn), lambda j: (0, base + j))
    return pl.pallas_call(
        functools.partial(partial_kernel, tile),
        grid=(width // bn,),
        in_specs=[pl.BlockSpec(memory_space=pltpu.SMEM), wide, whole, whole,
                  pl.BlockSpec((bn, rank), lambda j: (base + j, 0)), wide,
                  pl.BlockSpec((rank, m), lambda j: (0, 0))],
        out_specs=pl.BlockSpec((rank, bn), lambda j: (0, j)),
        out_shape=jax.ShapeDtypeStruct((rank, width), bf16),
        scratch_shapes=[pltpu.VMEM((rank, bn), f32)],
        compiler_params=pltpu.CompilerParams(vmem_limit_bytes=48 * MB),
        cost_estimate=pl.CostEstimate(flops=6 * m * width * rank, bytes_accessed=4 * m * width, transcendentals=0),
        name="partial_pass",
    )(s, w, left, descent, right, f, new_t)


def last_kernel(tile, s_ref, w_ref, l_ref, d_ref, r_ref, n_ref, q_ref, o_ref):
    s = s_ref[0, 0]
    s2 = s_ref[0, 1]
    m = l_ref.shape[0]

    def step_rows(i):
        rows = span(i, tile)
        early = lax.dot_general(l_ref[rows, :], r_ref[...], NT, preferred_element_type=f32)
        image = lax.dot_general(d_ref[rows, :], r_ref[...], NT, preferred_element_type=f32)
        second = jnp.dot(n_ref[rows, :], q_ref[...], preferred_element_type=f32)
        later = (w_ref[rows, :].astype(f32) - early) - s * image
        o_ref[rows, :] = (later - s2 * second).astype(o_ref.dtype)
    each(m // tile, UNROLL, step_rows)


def last_pass(steps, w, left, descent, right, left_new, right_t, block=512, tile=512):
    m, n = w.shape
    rank = left.shape[1]
    bn = pick(n, block)
    tile = pick(m, tile)
    whole = pl.BlockSpec((m, rank), lambda j: (0, 0))
    wide = pl.BlockSpec((m, bn), lambda j: (0, j))
    return pl.pallas_call(
        functools.partial(last_kernel, tile),
        grid=(n // bn,),
        in_specs=[pl.BlockSpec(memory_space=pltpu.SMEM), wide, whole, whole,
                  pl.BlockSpec((bn, rank), lambda j: (j, 0)), whole,
                  pl.BlockSpec((rank, bn), lambda j: (0, j))],
        out_specs=wide,
        out_shape=jax.ShapeDtypeStruct((m, n), bf16),
        compiler_params=pltpu.CompilerParams(vmem_limit_bytes=48 * MB),
        cost_estimate=pl.CostEstimate(flops=6 * m * n * rank, bytes_accessed=4 * m * n, transcendentals=0),
        name="last_pass",
    )(steps, w, left, descent, right, left_new, right_t)


epsilon = 1e-06


def cut(extent, weights):
    units = extent // 128 if extent % 128 == 0 else 1
    size = extent // units
    total = sum(weights)
    edges = [0]
    seen = 0
    for weight in weights:
        seen += weight
        edges.append(units * seen // total)
    return [(a * size, (b - a) * size) for a, b in zip(edges, edges[1:]) if b > a]


def other(count, bit):
    return [(i, i ^ bit) for i in range(count)]


def turned(count, by):
    return [(i, (i + by) % count) for i in range(count)]


def add_up(x, axis):
    count = lax.axis_size(axis)
    if count == 4:
        one, two, three = (lax.ppermute(x, axis, turned(4, k)) for k in (1, 2, 3))
        return (x + two) + (one + three)
    if count & (count - 1):
        return lax.psum(x, axis)
    bit = 1
    while bit < count:
        x = x + lax.ppermute(x, axis, other(count, bit))
        bit *= 2
    return x


def gather_line(own, axis):
    at = lax.axis_index(axis)
    outer = lax.ppermute(own, axis, [(0, 1), (1, 0), (2, 3), (3, 2)])
    pair = jnp.concatenate([own, outer], axis=0)
    middle = lax.ppermute(pair, axis, [(1, 2), (2, 1)])
    far = lax.ppermute(middle, axis, [(1, 0), (2, 3)])
    return [[own], [outer], [middle, far]]


def line_order(axis):
    at = lax.axis_index(axis)
    low = at < 2
    return [at, at ^ 1, jnp.where(low, 2, 1), jnp.where(low, 3, 0)]


def sum_line(x, axis):
    at = lax.axis_index(axis)
    inner = (at == 1) | (at == 2)
    came = lax.ppermute(x, axis, [(0, 1), (3, 2)])
    half = (x.astype(f32) + came.astype(f32)).astype(x.dtype)
    across = lax.ppermute(half, axis, [(1, 2), (2, 1)])
    total = (half.astype(f32) + across.astype(f32)).astype(x.dtype)
    back = lax.ppermute(total, axis, [(1, 0), (2, 3)])
    return jnp.where(inner, total, back)


def sum_columns(x, axis):
    count = lax.axis_size(axis)
    if count != 4 or x.shape[0] % 32:
        return lax.psum(x, axis)
    side = lax.axis_index(axis) & 1
    half = x.shape[0] // 2
    mine = lax.dynamic_slice_in_dim(x, side * half, half, 0)
    theirs = lax.dynamic_slice_in_dim(x, (1 - side) * half, half, 0)
    chip = (mine + lax.ppermute(theirs, axis, other(4, 1))).astype(bf16)
    both = chip.astype(f32) + lax.ppermute(chip, axis, other(4, 2)).astype(f32)
    rest = lax.ppermute(both, axis, other(4, 1))
    first = jnp.where(side == 0, both, rest)
    second = jnp.where(side == 0, rest, both)
    return jnp.concatenate([first, second], axis=0)


def ratio(pair):
    return jnp.sum(pair[1]) / (jnp.sum(pair[0]) + epsilon)


def body(activations, out_grads, matrix, left, right):
    col_count = lax.axis_size("col")
    row_count = lax.axis_size("row")
    m, n = matrix.shape
    shard = out_grads.shape[0]
    gathered = lax.all_gather(activations, "col", axis=0, tiled=True)
    if row_count == 4:
        blocks = gathered.reshape(row_count, shard, m)
        ordered = jnp.concatenate([lax.dynamic_index_in_dim(blocks, k, 0, False) for k in line_order("row")], axis=0)
        at = ordered.T
        pieces = []
        for offset, width in cut(n, (2, 2, 1, 1)):
            own = lax.slice_in_dim(out_grads, offset, offset + width, axis=1)
            pieces.append((offset, width, gather_line(own, "row")))
    else:
        at = gathered.T
        pieces = [(0, n, [[lax.all_gather(out_grads, "row", axis=0, tiled=True)]])]
    prev = None
    for offset, width, groups in pieces:
        fisher, partial = first_pass(at, matrix, left, right, groups, offset, width, prev, BLOCK, TILE)
        prev = (fisher, partial)
    left_descent = sum_columns(partial, "col")
    left_round = left_descent.astype(bf16)
    curve = curve_pass(left_round, right, fisher, 0, n, True, 2 * BLOCK, TILE)
    sums = jnp.stack([curve, fold(left_descent * left_descent) / col_count])
    left_step = ratio(add_up(add_up(sums, "col"), "row"))
    left_new = (left.astype(f32) + left_step * left_descent).astype(bf16)
    new_t = left_new.T
    right_parts = []
    curve = jnp.zeros((8, 128), f32)
    norm = jnp.zeros((8, 128), f32)
    for offset, width in cut(n, (1, 2, 2, 1)):
        part = partial_pass(left_step.reshape(1, 1), matrix, left, left_round, right, fisher, new_t, offset, width, BLOCK, TILE)
        total = sum_line(part, "row") if row_count == 4 else lax.psum(part, "row")
        curve = curve + curve_pass(left_new, total, fisher, offset, width, False, BLOCK, TILE)
        wide = total.astype(f32)
        norm = norm + fold(wide * wide)
        right_parts.append(total)
    right_t = jnp.concatenate(right_parts, axis=1)
    descent = right_t.T.astype(f32)
    right_step = ratio(add_up(add_up(jnp.stack([curve, norm / row_count]), "col"), "row"))
    steps = jnp.stack([left_step, right_step]).reshape(1, 2)
    residual = last_pass(steps, matrix, left, left_round, right, left_new, right_t, BLOCK, TILE)
    right_new = (right.astype(f32) + right_step * descent).astype(bf16)
    return (left_new, right_new, residual)


def solution(mesh):
    placed = (
        P(("grp", "col"), "row"),
        P(("grp", "row"), "col"),
        P(("grp", "row"), "col"),
        P(("grp", "row"), None),
        P(("grp", "col"), None),
    )
    return jax.shard_map(
        body,
        mesh=mesh,
        in_specs=placed,
        out_specs=(P(("grp", "row"), None), P(("grp", "col"), None), P(("grp", "row"), "col")),
        check_vma=False,
    )
```

```python
import functools
import math
import jax
import jax.numpy as jnp
from jax import lax
from jax.experimental import pallas as pl
from jax.experimental.pallas import tpu as pltpu
from jax.sharding import PartitionSpec as P

f32 = jnp.float32
bf16 = jnp.bfloat16
NT = (((1,), (1,)), ((), ()))
epsilon = 1e-06
BLOCK = 768
WIDE = 1152
TILE = 768
MB = 1 << 20


def pick(extent, want, offset=0):
    for size in range(min(want, extent), 0, -1):
        if extent % size == 0 and offset % size == 0 and (size % 128 == 0 or size == extent):
            return size
    return extent


def each(count, unroll, step):
    if unroll:
        for i in range(count):
            step(i)
    else:
        pl.loop(0, count)(step)


def span(i, tile):
    return pl.ds(i * tile, tile) if isinstance(i, int) else pl.ds(pl.multiple_of(i * tile, tile), tile)


UNROLL = True


def fold(x):
    rows, cols = x.shape
    y = x.reshape(rows // 8, 8, cols).sum(axis=0)
    out = y[:, :128]
    for at in range(128, cols, 128):
        out = out + y[:, at:at + 128]
    return out


def first_kernel(groups, tile, has_prev, *refs):
    at_ref, w_ref, l_ref, r_ref = refs[:4]
    used = 4
    parts = []
    for count in groups:
        parts.append(refs[used:used + count])
        used += count
    if has_prev:
        acc_in = refs[used]
        used += 2
    f_ref, acc_ref, g_ref = refs[used:used + 3]
    step = pl.program_id(0)
    at = 0
    for part in parts:
        total = part[0][...]
        for more in part[1:]:
            total = total + more[...]
        g_ref[pl.ds(at, total.shape[0]), :] = total
        at += total.shape[0]

    @pl.when(step == 0)
    def _():
        if has_prev:
            acc_ref[...] = acc_in[...]
        else:
            acc_ref[...] = jnp.zeros_like(acc_ref)

    m = at_ref.shape[0]

    def step_rows(i):
        rows = span(i, tile)
        grad = jnp.dot(at_ref[rows, :], g_ref[...], preferred_element_type=f32)
        image = lax.dot_general(l_ref[rows, :], r_ref[...], NT, preferred_element_type=f32)
        w = w_ref[rows, :].astype(f32)
        x = w * grad
        fisher = 1.0 + x * x
        f_ref[rows, :] = fisher.astype(f_ref.dtype)
        weighted = (fisher * (w - image)).astype(bf16)
        acc_ref[rows, :] += jnp.dot(weighted, r_ref[...], preferred_element_type=f32)
    each(m // tile, UNROLL, step_rows)


def first_pass(at, w, left, right, groups, offset, width, prev, block=512, tile=512, fdt=bf16):
    m, n = w.shape
    rank = left.shape[1]
    tokens = at.shape[1]
    bn = pick(width, block, offset)
    tile = pick(m, tile)
    base = offset // bn
    flat = [p for g in groups for p in g]
    ins = [at, w, left, right] + [p[0] for p in flat]

    def piece(array, rows, row, whole):
        shift = base if whole else 0
        return pl.BlockSpec((rows, bn), lambda j: (row, shift + j))

    specs = [
        pl.BlockSpec((m, tokens), lambda j: (0, 0)),
        pl.BlockSpec((m, bn), lambda j: (0, base + j)),
        pl.BlockSpec((m, rank), lambda j: (0, 0)),
        pl.BlockSpec((bn, rank), lambda j: (base + j, 0)),
    ] + [piece(*p) for p in flat]
    alias = {}
    if prev is not None:
        fprev, accprev = prev
        alias = {len(ins): 1, len(ins) + 1: 0}
        ins += [accprev, fprev]
        specs += [pl.BlockSpec((m, rank), lambda j: (0, 0)), pl.BlockSpec(memory_space=pl.ANY)]
    cost = pl.CostEstimate(flops=2 * m * width * (tokens + 2 * rank), bytes_accessed=m * width * 4, transcendentals=0)
    return pl.pallas_call(
        functools.partial(first_kernel, tuple(len(g) for g in groups), tile, prev is not None),
        grid=(width // bn,),
        in_specs=specs,
        out_specs=[pl.BlockSpec((m, bn), lambda j: (0, base + j)), pl.BlockSpec((m, rank), lambda j: (0, 0))],
        out_shape=[jax.ShapeDtypeStruct((m, n), fdt), jax.ShapeDtypeStruct((m, rank), f32)],
        scratch_shapes=[pltpu.VMEM((tokens, bn), bf16)],
        input_output_aliases=alias,
        compiler_params=pltpu.CompilerParams(vmem_limit_bytes=48 * MB),
        cost_estimate=cost,
        name="first_pass",
    )(*ins)


def total_of(refs):
    if len(refs) == 4:
        return (refs[0][...] + refs[2][...]) + (refs[1][...] + refs[3][...])
    return refs[0][...]


def step_of(total, copies):
    curve = jnp.sum(total[0], axis=(0, 1), keepdims=True)
    norm = jnp.sum(total[1], axis=(0, 1), keepdims=True) * (1.0 / copies)
    return norm / (curve + epsilon)


def left_curve_kernel(tile, d_ref, r_ref, f_ref, o_ref, a_ref):
    m = d_ref.shape[0]

    @pl.when(pl.program_id(0) == 0)
    def _():
        d = d_ref[...]
        a_ref[...] = d.astype(bf16)
        o_ref[0] = jnp.zeros((8, 128), f32)
        o_ref[1] = fold(d * d)

    def step_rows(i):
        rows = span(i, tile)
        image = lax.dot_general(a_ref[rows, :], r_ref[...], NT, preferred_element_type=f32)
        o_ref[0] += fold(f_ref[rows, :].astype(f32) * (image * image))
    each(m // tile, UNROLL, step_rows)


def left_curve(descent, right, f):
    m, rank = descent.shape
    n = f.shape[1]
    bn = pick(n, 2 * BLOCK)
    return pl.pallas_call(
        functools.partial(left_curve_kernel, pick(m, TILE)),
        grid=(n // bn,),
        in_specs=[pl.BlockSpec((m, rank), lambda j: (0, 0)), pl.BlockSpec((bn, rank), lambda j: (j, 0)),
                  pl.BlockSpec((m, bn), lambda j: (0, j))],
        out_specs=pl.BlockSpec((2, 8, 128), lambda j: (0, 0, 0)),
        out_shape=jax.ShapeDtypeStruct((2, 8, 128), f32),
        scratch_shapes=[pltpu.VMEM((m, rank), bf16)],
        compiler_params=pltpu.CompilerParams(vmem_limit_bytes=48 * MB),
        cost_estimate=pl.CostEstimate(flops=2 * m * n * rank, bytes_accessed=2 * m * n, transcendentals=0),
        name="left_curve",
    )(descent, right, f)


def right_curve_kernel(tile, flag_ref, a_ref, t_ref, b_ref, f_ref, i_ref, o_ref, q_ref):
    m = a_ref.shape[0]
    own = flag_ref[0, 0] > 0
    q = jnp.where(own, t_ref[...].astype(f32), b_ref[...].astype(f32))
    q_ref[...] = q.astype(bf16)

    @pl.when(pl.program_id(0) == 0)
    def _():
        o_ref[...] = i_ref[...]

    o_ref[1] += fold(q * q)

    def step_rows(i):
        rows = span(i, tile)
        image = jnp.dot(a_ref[rows, :], q_ref[...], preferred_element_type=f32)
        o_ref[0] += fold(f_ref[rows, :].astype(f32) * (image * image))
    each(m // tile, UNROLL, step_rows)


def right_curve(flag, left_new, total, back, f, sums, offset, width):
    m, rank = left_new.shape
    bn = pick(width, 2 * BLOCK, offset)
    base = offset // bn
    tall = pl.BlockSpec((rank, bn), lambda j: (0, j))
    small = pl.BlockSpec((2, 8, 128), lambda j: (0, 0, 0))
    return pl.pallas_call(
        functools.partial(right_curve_kernel, pick(m, TILE)),
        grid=(width // bn,),
        in_specs=[pl.BlockSpec(memory_space=pltpu.SMEM), pl.BlockSpec((m, rank), lambda j: (0, 0)), tall, tall,
                  pl.BlockSpec((m, bn), lambda j: (0, base + j)), small],
        out_specs=[small, tall],
        out_shape=[jax.ShapeDtypeStruct((2, 8, 128), f32), jax.ShapeDtypeStruct((rank, width), bf16)],
        compiler_params=pltpu.CompilerParams(vmem_limit_bytes=48 * MB),
        cost_estimate=pl.CostEstimate(flops=2 * m * width * rank, bytes_accessed=2 * m * width, transcendentals=0),
        name="right_curve",
    )(flag, left_new, total, back, f, sums)


def left_new_kernel(copies, *refs):
    l_ref, d_ref = refs[:2]
    step_ref, new_ref, t_ref, pair_ref = refs[-4:]
    rank = l_ref.shape[1]
    step = step_of(total_of(refs[2:-4]), copies)
    step_ref[...] = jnp.broadcast_to(step, (8, 128))
    left = l_ref[...].astype(f32)
    descent = d_ref[...]
    new = left + step * descent
    new_ref[...] = new.astype(bf16)
    t_ref[...] = new.T.astype(bf16)
    moved = left + step * descent.astype(bf16).astype(f32)
    high = moved.astype(bf16)
    pair_ref[:, :rank] = high
    pair_ref[:, rank:] = (moved - high.astype(f32)).astype(bf16)


def left_update(left, descent, pieces, copies):
    m, rank = left.shape
    return pl.pallas_call(
        functools.partial(left_new_kernel, copies),
        out_shape=[jax.ShapeDtypeStruct((8, 128), f32), jax.ShapeDtypeStruct((m, rank), bf16), jax.ShapeDtypeStruct((rank, m), bf16),
                   jax.ShapeDtypeStruct((m, 2 * rank), bf16)],
        compiler_params=pltpu.CompilerParams(vmem_limit_bytes=32 * MB),
        cost_estimate=pl.CostEstimate(flops=2 * m * rank, bytes_accessed=10 * m * rank, transcendentals=0),
        name="left_update",
    )(left, descent, *pieces)


def partial_kernel(tile, p_ref, w_ref, r_ref, f_ref, t_ref, k_ref, o_ref, acc_ref):
    m = p_ref.shape[0]
    acc_ref[...] = jnp.zeros_like(acc_ref)

    def step_rows(i):
        rows = span(i, tile)
        image = lax.dot_general(p_ref[rows, :], r_ref[...], NT, preferred_element_type=f32)
        later = w_ref[rows, :].astype(f32) - image
        weighted = (f_ref[rows, :].astype(f32) * later).astype(bf16)
        acc_ref[...] += jnp.dot(t_ref[:, rows], weighted, preferred_element_type=f32)
    each(m // tile, UNROLL, step_rows)
    o_ref[...] = acc_ref[...].astype(o_ref.dtype)


def partial_pass(pair, w, twice, f, new_t, token, offset, width):
    m, n = w.shape
    rank = new_t.shape[0]
    bn = pick(width, WIDE, offset)
    base = offset // bn
    tile = pick(m, TILE)
    wide = pl.BlockSpec((m, bn), lambda j: (0, base + j))
    return pl.pallas_call(
        functools.partial(partial_kernel, tile),
        grid=(width // bn,),
        in_specs=[pl.BlockSpec((m, 2 * rank), lambda j: (0, 0)), wide,
                  pl.BlockSpec((bn, 2 * rank), lambda j: (base + j, 0)), wide,
                  pl.BlockSpec((rank, m), lambda j: (0, 0)), pl.BlockSpec(memory_space=pl.ANY)],
        out_specs=pl.BlockSpec((rank, bn), lambda j: (0, j)),
        out_shape=jax.ShapeDtypeStruct((rank, width), bf16),
        scratch_shapes=[pltpu.VMEM((rank, bn), f32)],
        compiler_params=pltpu.CompilerParams(vmem_limit_bytes=48 * MB),
        cost_estimate=pl.CostEstimate(flops=6 * m * width * rank, bytes_accessed=4 * m * width, transcendentals=0),
        name="partial_pass",
    )(pair, w, twice, f, new_t, token)


def last_kernel(tile, copies, edges, *refs):
    w_ref, p_ref, r_ref, n_ref = refs[:4]
    q_refs = refs[4:4 + len(edges)]
    pieces = refs[4 + len(edges):-3]
    o_ref, new_ref, q_ref = refs[-3:]
    j = pl.program_id(0)
    s2 = step_of(total_of(pieces), copies)
    m = p_ref.shape[0]
    rank = n_ref.shape[1]
    for (first, count), ref in zip(edges, q_refs):
        @pl.when((j >= first) & (j < first + count))
        def _():
            q_ref[...] = ref[...]

    def step_rows(i):
        rows = span(i, tile)
        image = lax.dot_general(p_ref[rows, :], r_ref[...], NT, preferred_element_type=f32)
        second = jnp.dot(n_ref[rows, :], q_ref[...], preferred_element_type=f32)
        later = w_ref[rows, :].astype(f32) - image
        o_ref[rows, :] = (later - s2 * second).astype(o_ref.dtype)
    each(m // tile, UNROLL, step_rows)
    new_ref[...] = (r_ref[:, :rank].astype(f32) + s2 * q_ref[...].astype(f32).T).astype(bf16)


def last_pass(w, pair, twice, left_new, parts, pieces, copies):
    m, n = w.shape
    rank = left_new.shape[1]
    common = n
    at = 0
    edges = []
    for part in parts:
        common = math.gcd(common, part.shape[1])
    bn = pick(common, BLOCK)
    for part in parts:
        edges.append((at // bn, part.shape[1] // bn))
        at += part.shape[1]
    whole = pl.BlockSpec((m, rank), lambda j: (0, 0))
    wide = pl.BlockSpec((m, bn), lambda j: (0, j))
    side = pl.BlockSpec((bn, rank), lambda j: (j, 0))

    def tall(first, count):
        return pl.BlockSpec((rank, bn), lambda j: (0, jnp.clip(j - first, 0, count - 1)))

    return pl.pallas_call(
        functools.partial(last_kernel, pick(m, TILE), copies, tuple(edges)),
        grid=(n // bn,),
        in_specs=[wide, pl.BlockSpec((m, 2 * rank), lambda j: (0, 0)), pl.BlockSpec((bn, 2 * rank), lambda j: (j, 0)), whole]
        + [tall(*edge) for edge in edges]
        + [pl.BlockSpec((2, 8, 128), lambda j: (0, 0, 0))] * len(pieces),
        out_specs=[wide, side],
        out_shape=[jax.ShapeDtypeStruct((m, n), bf16), jax.ShapeDtypeStruct((n, rank), bf16)],
        scratch_shapes=[pltpu.VMEM((rank, bn), bf16)],
        compiler_params=pltpu.CompilerParams(vmem_limit_bytes=48 * MB),
        cost_estimate=pl.CostEstimate(flops=6 * m * n * rank, bytes_accessed=4 * m * n, transcendentals=0),
        name="last_pass",
    )(w, pair, twice, left_new, *parts, *pieces)


FIRST = (3, 2, 1)
SECOND = (1, 1, 1, 1)
ORDER = (
    ("p", 0), ("p", 1), ("p", 2), ("h", 0), ("p", 3), ("h", 1), ("t", 0), ("h", 2), ("t", 1),
    ("h", 3), ("v", 0), ("t", 2), ("v", 1), ("t", 3), ("v", 2), ("v", 3),
)


def cut(extent, weights):
    units = extent // 128 if extent % 128 == 0 else 1
    size = extent // units
    total = sum(weights)
    edges = [0]
    seen = 0
    for weight in weights:
        seen += weight
        edges.append(units * seen // total)
    return [(a * size, (b - a) * size) for a, b in zip(edges, edges[1:]) if b > a]


def other(count, bit):
    return [(i, i ^ bit) for i in range(count)]


def turned(count, by):
    return [(i, (i + by) % count) for i in range(count)]


def pieces_of(x, axis):
    if lax.axis_size(axis) == 4:
        return [x] + [lax.ppermute(x, axis, turned(4, k)) for k in (1, 2, 3)]
    return [add_up(x, axis)]


def add_up(x, axis):
    count = lax.axis_size(axis)
    if count == 4:
        own, one, two, three = pieces_of(x, axis)
        return (own + two) + (one + three)
    if count & (count - 1):
        return lax.psum(x, axis)
    bit = 1
    while bit < count:
        x = x + lax.ppermute(x, axis, other(count, bit))
        bit *= 2
    return x


def line_order(axis):
    at = lax.axis_index(axis)
    low = at < 2
    return [at, at ^ 1, jnp.where(low, 2, 1), jnp.where(low, 3, 0)]


def gather_blocks(x, axis):
    far = lax.ppermute(x, axis, other(4, 2))
    near = lax.ppermute(x, axis, other(4, 1))
    both = lax.ppermute(far, axis, other(4, 1))
    return jnp.stack([x, near, far, both])


def sum_columns(x, axis):
    count = lax.axis_size(axis)
    if count != 4 or x.shape[0] % 32:
        return lax.psum(x, axis)
    side = lax.axis_index(axis) & 1
    half = x.shape[0] // 2
    mine = lax.dynamic_slice_in_dim(x, side * half, half, 0)
    theirs = lax.dynamic_slice_in_dim(x, (1 - side) * half, half, 0)
    chip = (mine + lax.ppermute(theirs, axis, other(4, 1))).astype(bf16)
    both = chip.astype(f32) + lax.ppermute(chip, axis, other(4, 2)).astype(f32)
    rest = lax.ppermute(both, axis, other(4, 1))
    first = jnp.where(side == 0, both, rest)
    second = jnp.where(side == 0, rest, both)
    return jnp.concatenate([first, second], axis=0)


def after(x, *others):
    return lax.optimization_barrier((x,) + others)[0]


def right_sum(make, finish, chunks, axis):
    count = len(chunks)
    sent = [None] * count
    halves = [None] * count
    totals = [None] * count
    backs = [None] * count
    token = None

    def part(k):
        nonlocal token
        sent[k] = make(k, token)
        token = sent[k]

    def half(k):
        nonlocal token
        came = lax.ppermute(sent[k], axis, [(0, 1), (3, 2)])
        mine = after(sent[k], token)
        token = halves[k] = (mine.astype(f32) + came.astype(f32)).astype(mine.dtype)

    def total(k):
        nonlocal token
        across = lax.ppermute(halves[k], axis, [(1, 2), (2, 1)])
        mine = after(halves[k], token)
        token = totals[k] = (mine.astype(f32) + across.astype(f32)).astype(mine.dtype)

    def back(k):
        nonlocal token
        backs[k] = lax.ppermute(totals[k], axis, [(1, 0), (2, 3)])
        token = finish(k, totals[k], backs[k], token)

    for name, k in ORDER:
        (part, half, total, back)["phtv".index(name)](k)


def body(activations, out_grads, matrix, left, right):
    col_count = lax.axis_size("col")
    row_count = lax.axis_size("row")
    m, n = matrix.shape
    shard = out_grads.shape[0]
    line = row_count == 4 and col_count == 4
    twice = jnp.concatenate([right, right], axis=1)
    prev = None
    if line:
        outward = [(0, 1), (1, 0), (2, 3), (3, 2)]
        across = [(1, 2), (2, 1)]
        onward = [(1, 0), (2, 3)]
        outer = lax.ppermute(out_grads, "row", outward)
        inner = lax.ppermute(out_grads, "row", across)
        blocks = gather_blocks(activations, "col")
        me = lax.axis_index("col")
        ordered = jnp.concatenate([lax.dynamic_index_in_dim(blocks, k ^ me, 0, False) for k in line_order("row")], axis=0)
        at = ordered.T
        chunks = cut(n, FIRST)
        outers = [lax.slice_in_dim(outer, o, o + k, axis=1) for o, k in chunks]
        inners = [lax.slice_in_dim(inner, o, o + k, axis=1) for o, k in chunks]
        crossed = [lax.ppermute(x, "row", across) for x in outers]
        partials = []
        for k, (offset, width) in enumerate(chunks):
            if k == 0:
                early = lax.ppermute(inners[0], "row", onward)
                late = lax.ppermute(after(crossed[0], early), "row", onward)
                ends = [(early, shard, 0, False), (late, shard, 0, False)]
            else:
                both = jnp.concatenate([inners[k], crossed[k]], axis=0)
                both = after(both, at if k == 1 else partials[k - 2])
                end = lax.ppermute(both, "row", onward)
                ends = [(end, shard, 0, False), (end, shard, 1, False)]
            groups = [[(out_grads, shard, 0, True)], [(outer, shard, 0, True)],
                      [(inner, shard, 0, True), ends[0]], [(crossed[k], shard, 0, False), ends[1]]]
            prev = first_pass(at, matrix, left, right, groups, offset, width, prev, BLOCK, TILE)
            partials.append(prev[1])
    else:
        gathered = lax.all_gather(activations, "col", axis=0, tiled=True)
        grads = lax.all_gather(out_grads, "row", axis=0, tiled=True)
        prev = first_pass(gathered.T, matrix, left, right, [[(grads, grads.shape[0], 0, True)]], 0, n, None, BLOCK, TILE)
    fisher, partial = prev
    left_descent = sum_columns(partial, "col")
    sums = left_curve(left_descent, right, fisher)
    pieces = pieces_of(add_up(sums, "col"), "row")
    step, left_new, new_t, pair = left_update(left, left_descent, pieces, col_count)
    central = (lax.axis_index("row") % 3 != 0) if line else True
    flag = jnp.full((1, 1), central, jnp.int32)
    chunks = cut(n, SECOND)
    sums = jnp.zeros((2, 8, 128), f32)
    parts = [None] * len(chunks)

    def make(k, token):
        return partial_pass(pair, matrix, twice, fisher, new_t, step if token is None else token, *chunks[k])

    def finish(k, total, back, token):
        nonlocal sums
        if token is not None:
            total = after(total, token)
        sums, parts[k] = right_curve(flag, left_new, total, back, fisher, sums, *chunks[k])
        return sums

    if line:
        right_sum(make, finish, chunks, "row")
    else:
        for k in range(len(chunks)):
            total = lax.psum(make(k, None), "row")
            finish(k, total, total, None)
    pieces = pieces_of(add_up(sums, "col"), "row")
    residual, right_new = last_pass(matrix, pair, twice, left_new, parts, pieces, row_count)
    return (left_new, right_new, residual)


def solution(mesh):
    placed = (
        P(("grp", "col"), "row"),
        P(("grp", "row"), "col"),
        P(("grp", "row"), "col"),
        P(("grp", "row"), None),
        P(("grp", "col"), None),
    )
    return jax.shard_map(
        body,
        mesh=mesh,
        in_specs=placed,
        out_specs=(P(("grp", "row"), None), P(("grp", "col"), None), P(("grp", "row"), "col")),
        check_vma=False,
    )
```

```python
import functools
import math
import jax
import jax.numpy as jnp
from jax import lax
from jax.experimental import pallas as pl
from jax.experimental.pallas import tpu as pltpu
from jax.sharding import PartitionSpec as P

f32 = jnp.float32
bf16 = jnp.bfloat16
NT = (((1,), (1,)), ((), ()))
epsilon = 1e-06
BLOCK = 768
WIDE = 384
TILE = 768
MB = 1 << 20
LIMIT = 48 * MB


def near(x):
    return pltpu.with_memory_space_constraint(x, pltpu.VMEM)


def far(x):
    return pltpu.with_memory_space_constraint(x, pltpu.HBM)


def pick(extent, want, offset=0):
    for size in range(min(want, extent), 0, -1):
        if extent % size == 0 and offset % size == 0 and (size % 128 == 0 or size == extent):
            return size
    return extent


def each(count, unroll, step):
    if unroll:
        for i in range(count):
            step(i)
    else:
        pl.loop(0, count)(step)


def span(i, tile):
    return pl.ds(i * tile, tile) if isinstance(i, int) else pl.ds(pl.multiple_of(i * tile, tile), tile)


UNROLL = True


def fold(x):
    rows, cols = x.shape
    y = x.reshape(rows // 8, 8, cols).sum(axis=0)
    out = y[:, :128]
    for at in range(128, cols, 128):
        out = out + y[:, at:at + 128]
    return out


def first_kernel(groups, tile, has_prev, *refs):
    at_ref, w_ref, l_ref, r_ref = refs[:4]
    used = 4
    parts = []
    for count in groups:
        parts.append(refs[used:used + count])
        used += count
    if has_prev:
        acc_in = refs[used]
        used += 2
    f_ref, acc_ref, g_ref = refs[used:used + 3]
    step = pl.program_id(0)
    at = 0
    for part in parts:
        total = part[0][...]
        for more in part[1:]:
            total = total + more[...]
        g_ref[pl.ds(at, total.shape[0]), :] = total
        at += total.shape[0]

    @pl.when(step == 0)
    def _():
        if has_prev:
            acc_ref[...] = acc_in[...]
        else:
            acc_ref[...] = jnp.zeros_like(acc_ref)

    m = at_ref.shape[0]

    def step_rows(i):
        rows = span(i, tile)
        grad = jnp.dot(at_ref[rows, :], g_ref[...], preferred_element_type=f32)
        image = lax.dot_general(l_ref[rows, :], r_ref[...], NT, preferred_element_type=f32)
        w = w_ref[rows, :].astype(f32)
        x = w * grad
        fisher = 1.0 + x * x
        f_ref[rows, :] = fisher.astype(f_ref.dtype)
        weighted = (fisher * (w - image)).astype(bf16)
        acc_ref[rows, :] += jnp.dot(weighted, r_ref[...], preferred_element_type=f32)
    each(m // tile, UNROLL, step_rows)


def first_pass(at, w, left, right, groups, offset, width, prev, block=512, tile=512, fdt=bf16):
    m, n = w.shape
    rank = left.shape[1]
    tokens = at.shape[1]
    bn = pick(width, block, offset)
    tile = pick(m, tile)
    base = offset // bn
    flat = [p for g in groups for p in g]
    ins = [near(at), far(w), far(left), far(right)] + [far(p[0]) for p in flat]

    def piece(array, rows, row, whole):
        shift = base if whole else 0
        return pl.BlockSpec((rows, bn), lambda j: (row, shift + j))

    specs = [
        pl.BlockSpec((m, tokens), lambda j: (0, 0)),
        pl.BlockSpec((m, bn), lambda j: (0, base + j)),
        pl.BlockSpec((m, rank), lambda j: (0, 0)),
        pl.BlockSpec((bn, rank), lambda j: (base + j, 0)),
    ] + [piece(*p) for p in flat]
    alias = {}
    if prev is not None:
        fprev, accprev = prev
        alias = {len(ins): 1, len(ins) + 1: 0}
        ins += [near(accprev), far(fprev)]
        specs += [pl.BlockSpec((m, rank), lambda j: (0, 0)), pl.BlockSpec(memory_space=pl.ANY)]
    cost = pl.CostEstimate(flops=2 * m * width * (tokens + 2 * rank), bytes_accessed=m * width * 4, transcendentals=0)
    return pl.pallas_call(
        functools.partial(first_kernel, tuple(len(g) for g in groups), tile, prev is not None),
        grid=(width // bn,),
        in_specs=specs,
        out_specs=[pl.BlockSpec((m, bn), lambda j: (0, base + j)), pl.BlockSpec((m, rank), lambda j: (0, 0))],
        out_shape=[pltpu.HBM((m, n), fdt), pltpu.VMEM((m, rank), f32)],
        scratch_shapes=[pltpu.VMEM((tokens, bn), bf16)],
        input_output_aliases=alias,
        compiler_params=pltpu.CompilerParams(vmem_limit_bytes=LIMIT),
        cost_estimate=cost,
        name="first_pass",
    )(*ins)


def total_of(refs):
    if len(refs) == 4:
        return (refs[0][...] + refs[2][...]) + (refs[1][...] + refs[3][...])
    return refs[0][...]


def step_of(total, copies):
    curve = jnp.sum(total[0], axis=(0, 1), keepdims=True)
    norm = jnp.sum(total[1], axis=(0, 1), keepdims=True) * (1.0 / copies)
    return norm / (curve + epsilon)


def left_curve_kernel(tile, side_ref, b_ref, c_ref, r_ref, f_ref, o_ref, d_ref, a_ref):
    m = d_ref.shape[0]
    half = m // 2

    @pl.when(pl.program_id(0) == 0)
    def _():
        low = side_ref[0, 0] == 0
        total = jnp.zeros((8, 128), f32)
        for at, first, second in ((0, b_ref, c_ref), (half, c_ref, b_ref)):
            d = jnp.where(low, first[...], second[...])
            d_ref[pl.ds(at, half), :] = d
            a_ref[pl.ds(at, half), :] = d.astype(bf16)
            total = total + fold(d * d)
        o_ref[0] = jnp.zeros((8, 128), f32)
        o_ref[1] = total

    def step_rows(i):
        rows = span(i, tile)
        image = lax.dot_general(a_ref[rows, :], r_ref[...], NT, preferred_element_type=f32)
        o_ref[0] += fold(f_ref[rows, :].astype(f32) * (image * image))
    each(m // tile, UNROLL, step_rows)


def left_curve(side, halves, right, f):
    m, n = f.shape
    rank = right.shape[1]
    bn = pick(n, 2 * BLOCK)
    half = pl.BlockSpec((m // 2, rank), lambda j: (0, 0))
    return pl.pallas_call(
        functools.partial(left_curve_kernel, pick(m, TILE)),
        grid=(n // bn,),
        in_specs=[pl.BlockSpec(memory_space=pltpu.SMEM), half, half, pl.BlockSpec((bn, rank), lambda j: (j, 0)),
                  pl.BlockSpec((m, bn), lambda j: (0, j))],
        out_specs=[pl.BlockSpec((2, 8, 128), lambda j: (0, 0, 0)), pl.BlockSpec((m, rank), lambda j: (0, 0))],
        out_shape=[jax.ShapeDtypeStruct((2, 8, 128), f32), pltpu.VMEM((m, rank), f32)],
        scratch_shapes=[pltpu.VMEM((m, rank), bf16)],
        compiler_params=pltpu.CompilerParams(vmem_limit_bytes=LIMIT),
        cost_estimate=pl.CostEstimate(flops=2 * m * n * rank, bytes_accessed=2 * m * n, transcendentals=0),
        name="left_curve",
    )(side, *halves, far(right), far(f))


def right_curve_kernel(tile, flag_ref, a_ref, t_ref, b_ref, f_ref, i_ref, o_ref, q_ref):
    m = a_ref.shape[0]
    own = flag_ref[0, 0] > 0
    q = jnp.where(own, t_ref[...].astype(f32), b_ref[...].astype(f32))
    q_ref[...] = q.astype(bf16)

    @pl.when(pl.program_id(0) == 0)
    def _():
        o_ref[...] = i_ref[...]

    o_ref[1] += fold(q * q)

    def step_rows(i):
        rows = span(i, tile)
        image = jnp.dot(a_ref[rows, :], q_ref[...], preferred_element_type=f32)
        o_ref[0] += fold(f_ref[rows, :].astype(f32) * (image * image))
    each(m // tile, UNROLL, step_rows)


def right_curve(flag, left_new, total, back, f, sums, offset, width):
    m, rank = left_new.shape
    bn = pick(width, 2 * BLOCK, offset)
    base = offset // bn
    tall = pl.BlockSpec((rank, bn), lambda j: (0, j))
    small = pl.BlockSpec((2, 8, 128), lambda j: (0, 0, 0))
    return pl.pallas_call(
        functools.partial(right_curve_kernel, pick(m, TILE)),
        grid=(width // bn,),
        in_specs=[pl.BlockSpec(memory_space=pltpu.SMEM), pl.BlockSpec((m, rank), lambda j: (0, 0)), tall, tall,
                  pl.BlockSpec((m, bn), lambda j: (0, base + j)), small],
        out_specs=[small, tall],
        out_shape=[jax.ShapeDtypeStruct((2, 8, 128), f32), jax.ShapeDtypeStruct((rank, width), bf16)],
        compiler_params=pltpu.CompilerParams(vmem_limit_bytes=LIMIT),
        cost_estimate=pl.CostEstimate(flops=2 * m * width * rank, bytes_accessed=2 * m * width, transcendentals=0),
        name="right_curve",
    )(flag, far(left_new), total, back, far(f), sums)


def left_new_kernel(copies, *refs):
    l_ref, d_ref = refs[:2]
    step_ref, new_ref, t_ref, pair_ref = refs[-4:]
    rank = l_ref.shape[1]
    step = step_of(total_of(refs[2:-4]), copies)
    step_ref[...] = jnp.broadcast_to(step, (8, 128))
    left = l_ref[...].astype(f32)
    descent = d_ref[...]
    new = left + step * descent
    new_ref[...] = new.astype(bf16)
    t_ref[...] = new.T.astype(bf16)
    moved = left + step * descent.astype(bf16).astype(f32)
    high = moved.astype(bf16)
    pair_ref[:, :rank] = high
    pair_ref[:, rank:] = (moved - high.astype(f32)).astype(bf16)


def left_update(left, descent, pieces, copies):
    m, rank = left.shape
    return pl.pallas_call(
        functools.partial(left_new_kernel, copies),
        out_shape=[jax.ShapeDtypeStruct((8, 128), f32), pltpu.HBM((m, rank), bf16), pltpu.VMEM((rank, m), bf16),
                   pltpu.VMEM((m, 2 * rank), bf16)],
        compiler_params=pltpu.CompilerParams(vmem_limit_bytes=LIMIT),
        cost_estimate=pl.CostEstimate(flops=2 * m * rank, bytes_accessed=10 * m * rank, transcendentals=0),
        name="left_update",
    )(far(left), near(descent), *pieces)


def partial_kernel(tile, p_ref, w_ref, r_ref, f_ref, t_ref, k_ref, o_ref, acc_ref):
    m = p_ref.shape[0]
    acc_ref[...] = jnp.zeros_like(acc_ref)

    def step_rows(i):
        rows = span(i, tile)
        image = lax.dot_general(p_ref[rows, :], r_ref[...], NT, preferred_element_type=f32)
        later = w_ref[rows, :].astype(f32) - image
        weighted = (f_ref[rows, :].astype(f32) * later).astype(bf16)
        acc_ref[...] += jnp.dot(t_ref[:, rows], weighted, preferred_element_type=f32)
    each(m // tile, UNROLL, step_rows)
    o_ref[...] = acc_ref[...].astype(o_ref.dtype)


def partial_pass(pair, w, twice, f, new_t, token, offset, width):
    m, n = w.shape
    rank = new_t.shape[0]
    bn = pick(width, WIDE, offset)
    base = offset // bn
    tile = pick(m, TILE)
    wide = pl.BlockSpec((m, bn), lambda j: (0, base + j))
    return pl.pallas_call(
        functools.partial(partial_kernel, tile),
        grid=(width // bn,),
        in_specs=[pl.BlockSpec((m, 2 * rank), lambda j: (0, 0)), wide,
                  pl.BlockSpec((bn, 2 * rank), lambda j: (base + j, 0)), wide,
                  pl.BlockSpec((rank, m), lambda j: (0, 0)), pl.BlockSpec(memory_space=pl.ANY)],
        out_specs=pl.BlockSpec((rank, bn), lambda j: (0, j)),
        out_shape=jax.ShapeDtypeStruct((rank, width), bf16),
        scratch_shapes=[pltpu.VMEM((rank, bn), f32)],
        compiler_params=pltpu.CompilerParams(vmem_limit_bytes=LIMIT),
        cost_estimate=pl.CostEstimate(flops=6 * m * width * rank, bytes_accessed=4 * m * width, transcendentals=0),
        name="partial_pass",
    )(near(pair), far(w), far(twice), far(f), near(new_t), token)


def last_kernel(tile, copies, edges, *refs):
    w_ref, p_ref, r_ref, n_ref = refs[:4]
    q_refs = refs[4:4 + len(edges)]
    pieces = refs[4 + len(edges):-3]
    o_ref, new_ref, q_ref = refs[-3:]
    j = pl.program_id(0)
    s2 = step_of(total_of(pieces), copies)
    m = p_ref.shape[0]
    rank = n_ref.shape[1]
    for (first, count), ref in zip(edges, q_refs):
        @pl.when((j >= first) & (j < first + count))
        def _():
            q_ref[...] = ref[...]

    def step_rows(i):
        rows = span(i, tile)
        image = lax.dot_general(p_ref[rows, :], r_ref[...], NT, preferred_element_type=f32)
        second = jnp.dot(n_ref[rows, :], q_ref[...], preferred_element_type=f32)
        later = w_ref[rows, :].astype(f32) - image
        o_ref[rows, :] = (later - s2 * second).astype(o_ref.dtype)
    each(m // tile, UNROLL, step_rows)
    new_ref[...] = (r_ref[:, :rank].astype(f32) + s2 * q_ref[...].astype(f32).T).astype(bf16)


def last_pass(w, pair, twice, left_new, parts, pieces, copies):
    m, n = w.shape
    rank = left_new.shape[1]
    common = n
    at = 0
    edges = []
    for part in parts:
        common = math.gcd(common, part.shape[1])
    bn = pick(common, 3 * BLOCK // 2)
    for part in parts:
        edges.append((at // bn, part.shape[1] // bn))
        at += part.shape[1]
    whole = pl.BlockSpec((m, rank), lambda j: (0, 0))
    wide = pl.BlockSpec((m, bn), lambda j: (0, j))
    side = pl.BlockSpec((bn, rank), lambda j: (j, 0))

    def tall(first, count):
        return pl.BlockSpec((rank, bn), lambda j: (0, jnp.clip(j - first, 0, count - 1)))

    return pl.pallas_call(
        functools.partial(last_kernel, pick(m, TILE), copies, tuple(edges)),
        grid=(n // bn,),
        in_specs=[wide, pl.BlockSpec((m, 2 * rank), lambda j: (0, 0)), pl.BlockSpec((bn, 2 * rank), lambda j: (j, 0)), whole]
        + [tall(*edge) for edge in edges]
        + [pl.BlockSpec((2, 8, 128), lambda j: (0, 0, 0))] * len(pieces),
        out_specs=[wide, side],
        out_shape=[jax.ShapeDtypeStruct((m, n), bf16), jax.ShapeDtypeStruct((n, rank), bf16)],
        scratch_shapes=[pltpu.VMEM((rank, bn), bf16)],
        compiler_params=pltpu.CompilerParams(vmem_limit_bytes=LIMIT),
        cost_estimate=pl.CostEstimate(flops=6 * m * n * rank, bytes_accessed=4 * m * n, transcendentals=0),
        name="last_pass",
    )(far(w), near(pair), far(twice), far(left_new), *parts, *pieces)


FIRST = (3, 2, 1)
SECOND = (1, 1, 1, 1)
ORDER = (
    ("p", 0), ("p", 1), ("p", 2), ("h", 0), ("p", 3), ("h", 1), ("t", 0), ("h", 2), ("t", 1),
    ("h", 3), ("v", 0), ("t", 2), ("v", 1), ("t", 3), ("v", 2), ("v", 3),
)


def cut(extent, weights):
    units = extent // 128 if extent % 128 == 0 else 1
    size = extent // units
    total = sum(weights)
    edges = [0]
    seen = 0
    for weight in weights:
        seen += weight
        edges.append(units * seen // total)
    return [(a * size, (b - a) * size) for a, b in zip(edges, edges[1:]) if b > a]


def other(count, bit):
    return [(i, i ^ bit) for i in range(count)]


def turned(count, by):
    return [(i, (i + by) % count) for i in range(count)]


def pieces_of(x, axis):
    if lax.axis_size(axis) == 4:
        return [x] + [lax.ppermute(x, axis, turned(4, k)) for k in (1, 2, 3)]
    return [add_up(x, axis)]


def add_up(x, axis):
    count = lax.axis_size(axis)
    if count == 4:
        own, one, two, three = pieces_of(x, axis)
        return (own + two) + (one + three)
    if count & (count - 1):
        return lax.psum(x, axis)
    bit = 1
    while bit < count:
        x = x + lax.ppermute(x, axis, other(count, bit))
        bit *= 2
    return x


def line_order(axis):
    at = lax.axis_index(axis)
    low = at < 2
    return [at, at ^ 1, jnp.where(low, 2, 1), jnp.where(low, 3, 0)]


def sum_columns(x, axis):
    count = lax.axis_size(axis)
    if count != 4 or x.shape[0] % 32:
        whole = lax.psum(x, axis)
        return whole[:x.shape[0] // 2], whole[x.shape[0] // 2:]
    side = lax.axis_index(axis) & 1
    half = x.shape[0] // 2
    mine = lax.dynamic_slice_in_dim(x, side * half, half, 0)
    theirs = lax.dynamic_slice_in_dim(x, (1 - side) * half, half, 0)
    chip = (mine + lax.ppermute(theirs, axis, other(4, 1))).astype(bf16)
    both = chip.astype(f32) + lax.ppermute(chip, axis, other(4, 2)).astype(f32)
    return both, lax.ppermute(both, axis, other(4, 1))


def after(x, *others):
    return lax.optimization_barrier((x,) + others)[0]


def right_sum(make, finish, chunks, axis):
    count = len(chunks)
    sent = [None] * count
    halves = [None] * count
    totals = [None] * count
    backs = [None] * count
    token = None

    def part(k):
        nonlocal token
        sent[k] = make(k, token)
        token = sent[k]

    def half(k):
        nonlocal token
        came = lax.ppermute(sent[k], axis, [(0, 1), (3, 2)])
        mine = after(sent[k], token)
        token = halves[k] = (mine.astype(f32) + came.astype(f32)).astype(mine.dtype)

    def total(k):
        nonlocal token
        across = lax.ppermute(halves[k], axis, [(1, 2), (2, 1)])
        mine = after(halves[k], token)
        token = totals[k] = (mine.astype(f32) + across.astype(f32)).astype(mine.dtype)

    def back(k):
        nonlocal token
        backs[k] = lax.ppermute(totals[k], axis, [(1, 0), (2, 3)])
        token = finish(k, totals[k], backs[k], token)

    for name, k in ORDER:
        (part, half, total, back)["phtv".index(name)](k)


def body(activations, out_grads, matrix, left, right):
    col_count = lax.axis_size("col")
    row_count = lax.axis_size("row")
    m, n = matrix.shape
    shard = out_grads.shape[0]
    line = row_count == 4 and col_count == 4
    twice = jnp.concatenate([right, right], axis=1)
    prev = None
    if line:
        outward = [(0, 1), (1, 0), (2, 3), (3, 2)]
        across = [(1, 2), (2, 1)]
        onward = [(1, 0), (2, 3)]
        outer = lax.ppermute(out_grads, "row", outward)
        inner = lax.ppermute(out_grads, "row", across)
        chunks = cut(n, FIRST)
        outers = [lax.slice_in_dim(outer, o, o + k, axis=1) for o, k in chunks]
        inners = [lax.slice_in_dim(inner, o, o + k, axis=1) for o, k in chunks]
        beside = lax.ppermute(activations, "col", other(4, 1))
        beyond = lax.ppermute(activations, "col", other(4, 2))
        crossed = [lax.ppermute(after(outers[0], beside, beyond), "row", across)]
        crossed += [lax.ppermute(after(x, crossed[0]), "row", across) for x in outers[1:]]
        corner = lax.ppermute(after(beyond, crossed[0]), "col", other(4, 1))
        blocks = jnp.stack([activations, beside, beyond, corner])
        me = lax.axis_index("col")
        ordered = jnp.concatenate([lax.dynamic_index_in_dim(blocks, k ^ me, 0, False) for k in line_order("row")], axis=0)
        at = ordered.T
        partials = []
        for k, (offset, width) in enumerate(chunks):
            if k == 0:
                early = lax.ppermute(inners[0], "row", onward)
                late = lax.ppermute(after(crossed[0], early), "row", onward)
                ends = [(early, shard, 0, False), (late, shard, 0, False)]
            else:
                both = jnp.concatenate([inners[k], crossed[k]], axis=0)
                both = after(both, at if k == 1 else partials[k - 2])
                end = lax.ppermute(both, "row", onward)
                ends = [(end, shard, 0, False), (end, shard, 1, False)]
            groups = [[(out_grads, shard, 0, True)], [(outer, shard, 0, True)],
                      [(inner, shard, 0, True), ends[0]], [(crossed[k], shard, 0, False), ends[1]]]
            prev = first_pass(at, matrix, left, right, groups, offset, width, prev, BLOCK, TILE)
            partials.append(prev[1])
    else:
        gathered = lax.all_gather(activations, "col", axis=0, tiled=True)
        grads = lax.all_gather(out_grads, "row", axis=0, tiled=True)
        prev = first_pass(gathered.T, matrix, left, right, [[(grads, grads.shape[0], 0, True)]], 0, n, None, BLOCK, TILE)
    fisher, partial = prev
    halves = sum_columns(partial, "col")
    side = lax.axis_index("col") & 1 if col_count == 4 else 0
    sums, left_descent = left_curve(jnp.full((1, 1), side, jnp.int32), halves, right, fisher)
    pieces = pieces_of(add_up(sums, "col"), "row")
    step, left_new, new_t, pair = left_update(left, left_descent, pieces, col_count)
    central = (lax.axis_index("row") % 3 != 0) if line else True
    flag = jnp.full((1, 1), central, jnp.int32)
    chunks = cut(n, SECOND)
    sums = jnp.zeros((2, 8, 128), f32)
    parts = [None] * len(chunks)

    def make(k, token):
        return partial_pass(pair, matrix, twice, fisher, new_t, step if token is None else token, *chunks[k])

    def finish(k, total, back, token):
        nonlocal sums
        if token is not None:
            total = after(total, token)
        sums, parts[k] = right_curve(flag, left_new, total, back, fisher, sums, *chunks[k])
        return sums

    if line:
        right_sum(make, finish, chunks, "row")
    else:
        for k in range(len(chunks)):
            total = lax.psum(make(k, None), "row")
            finish(k, total, total, None)
    pieces = pieces_of(add_up(sums, "col"), "row")
    residual, right_new = last_pass(matrix, pair, twice, left_new, parts, pieces, row_count)
    return (left_new, right_new, residual)


def solution(mesh):
    placed = (
        P(("grp", "col"), "row"),
        P(("grp", "row"), "col"),
        P(("grp", "row"), "col"),
        P(("grp", "row"), None),
        P(("grp", "col"), None),
    )
    return jax.shard_map(
        body,
        mesh=mesh,
        in_specs=placed,
        out_specs=(P(("grp", "row"), None), P(("grp", "col"), None), P(("grp", "row"), "col")),
        check_vma=False,
    )
```

```python
import functools
import math
import jax
import jax.numpy as jnp
from jax import lax
from jax.experimental import pallas as pl
from jax.experimental.pallas import tpu as pltpu
from jax.sharding import PartitionSpec as P

f32 = jnp.float32
bf16 = jnp.bfloat16
NT = (((1,), (1,)), ((), ()))
epsilon = 1e-06
BLOCK = 768
WIDE = 384
TILE = 768
MB = 1 << 20
LIMIT = 48 * MB


def near(x):
    return pltpu.with_memory_space_constraint(x, pltpu.VMEM)


def far(x):
    return pltpu.with_memory_space_constraint(x, pltpu.HBM)


def pick(extent, want, offset=0):
    for size in range(min(want, extent), 0, -1):
        if extent % size == 0 and offset % size == 0 and (size % 128 == 0 or size == extent):
            return size
    return extent


def each(count, unroll, step):
    if unroll:
        for i in range(count):
            step(i)
    else:
        pl.loop(0, count)(step)


def span(i, tile):
    return pl.ds(i * tile, tile) if isinstance(i, int) else pl.ds(pl.multiple_of(i * tile, tile), tile)


UNROLL = True


def fold(x):
    rows, cols = x.shape
    y = x.reshape(rows // 8, 8, cols).sum(axis=0)
    out = y[:, :128]
    for at in range(128, cols, 128):
        out = out + y[:, at:at + 128]
    return out


def first_kernel(groups, tile, has_prev, *refs):
    at_ref, w_ref, l_ref, r_ref = refs[:4]
    used = 4
    parts = []
    for count in groups:
        parts.append(refs[used:used + count])
        used += count
    if has_prev:
        acc_in = refs[used]
        used += 2
    f_ref, acc_ref, g_ref = refs[used:used + 3]
    step = pl.program_id(0)
    at = 0
    for part in parts:
        total = part[0][...]
        for more in part[1:]:
            total = total + more[...]
        g_ref[pl.ds(at, total.shape[0]), :] = total
        at += total.shape[0]

    @pl.when(step == 0)
    def _():
        if has_prev:
            acc_ref[...] = acc_in[...]
        else:
            acc_ref[...] = jnp.zeros_like(acc_ref)

    m = at_ref.shape[0]

    def step_rows(i):
        rows = span(i, tile)
        grad = jnp.dot(at_ref[rows, :], g_ref[...], preferred_element_type=f32)
        image = lax.dot_general(l_ref[rows, :], r_ref[...], NT, preferred_element_type=f32)
        w = w_ref[rows, :].astype(f32)
        x = w * grad
        fisher = 1.0 + x * x
        f_ref[rows, :] = fisher.astype(f_ref.dtype)
        weighted = (fisher * (w - image)).astype(bf16)
        acc_ref[rows, :] += jnp.dot(weighted, r_ref[...], preferred_element_type=f32)
    each(m // tile, UNROLL, step_rows)


def first_pass(at, w, left, right, groups, offset, width, prev, block=512, tile=512, fdt=bf16):
    m, n = w.shape
    rank = left.shape[1]
    tokens = at.shape[1]
    bn = pick(width, block, offset)
    tile = pick(m, tile)
    base = offset // bn
    flat = [p for g in groups for p in g]
    ins = [near(at), far(w), far(left), far(right)] + [far(p[0]) for p in flat]

    def piece(array, rows, row, whole):
        shift = base if whole else 0
        return pl.BlockSpec((rows, bn), lambda j: (row, shift + j))

    specs = [
        pl.BlockSpec((m, tokens), lambda j: (0, 0)),
        pl.BlockSpec((m, bn), lambda j: (0, base + j)),
        pl.BlockSpec((m, rank), lambda j: (0, 0)),
        pl.BlockSpec((bn, rank), lambda j: (base + j, 0)),
    ] + [piece(*p) for p in flat]
    alias = {}
    if prev is not None:
        fprev, accprev = prev
        alias = {len(ins): 1, len(ins) + 1: 0}
        ins += [near(accprev), far(fprev)]
        specs += [pl.BlockSpec((m, rank), lambda j: (0, 0)), pl.BlockSpec(memory_space=pl.ANY)]
    cost = pl.CostEstimate(flops=2 * m * width * (tokens + 2 * rank), bytes_accessed=m * width * 4, transcendentals=0)
    return pl.pallas_call(
        functools.partial(first_kernel, tuple(len(g) for g in groups), tile, prev is not None),
        grid=(width // bn,),
        in_specs=specs,
        out_specs=[pl.BlockSpec((m, bn), lambda j: (0, base + j)), pl.BlockSpec((m, rank), lambda j: (0, 0))],
        out_shape=[pltpu.HBM((m, n), fdt), pltpu.VMEM((m, rank), f32)],
        scratch_shapes=[pltpu.VMEM((tokens, bn), bf16)],
        input_output_aliases=alias,
        compiler_params=pltpu.CompilerParams(vmem_limit_bytes=LIMIT),
        cost_estimate=cost,
        name="first_pass",
    )(*ins)


def total_of(refs):
    if len(refs) == 4:
        return (refs[0][...] + refs[2][...]) + (refs[1][...] + refs[3][...])
    return refs[0][...]


def step_of(total, copies):
    curve = jnp.sum(total[0], axis=(0, 1), keepdims=True)
    norm = jnp.sum(total[1], axis=(0, 1), keepdims=True) * (1.0 / copies)
    return norm / (curve + epsilon)


def left_curve_kernel(tile, side_ref, b_ref, c_ref, r_ref, f_ref, o_ref, d_ref, a_ref):
    m = d_ref.shape[0]
    half = m // 2

    @pl.when(pl.program_id(0) == 0)
    def _():
        low = side_ref[0, 0] == 0
        total = jnp.zeros((8, 128), f32)
        for at, first, second in ((0, b_ref, c_ref), (half, c_ref, b_ref)):
            d = jnp.where(low, first[...], second[...])
            d_ref[pl.ds(at, half), :] = d
            a_ref[pl.ds(at, half), :] = d.astype(bf16)
            total = total + fold(d * d)
        o_ref[0] = jnp.zeros((8, 128), f32)
        o_ref[1] = total

    def step_rows(i):
        rows = span(i, tile)
        image = lax.dot_general(a_ref[rows, :], r_ref[...], NT, preferred_element_type=f32)
        o_ref[0] += fold(f_ref[rows, :].astype(f32) * (image * image))
    each(m // tile, UNROLL, step_rows)


def left_curve(side, halves, right, f):
    m, n = f.shape
    rank = right.shape[1]
    bn = pick(n, 3 * BLOCK)
    half = pl.BlockSpec((m // 2, rank), lambda j: (0, 0))
    return pl.pallas_call(
        functools.partial(left_curve_kernel, pick(m, TILE)),
        grid=(n // bn,),
        in_specs=[pl.BlockSpec(memory_space=pltpu.SMEM), half, half, pl.BlockSpec((bn, rank), lambda j: (j, 0)),
                  pl.BlockSpec((m, bn), lambda j: (0, j))],
        out_specs=[pl.BlockSpec((2, 8, 128), lambda j: (0, 0, 0)), pl.BlockSpec((m, rank), lambda j: (0, 0))],
        out_shape=[jax.ShapeDtypeStruct((2, 8, 128), f32), pltpu.VMEM((m, rank), f32)],
        scratch_shapes=[pltpu.VMEM((m, rank), bf16)],
        compiler_params=pltpu.CompilerParams(vmem_limit_bytes=LIMIT),
        cost_estimate=pl.CostEstimate(flops=2 * m * n * rank, bytes_accessed=2 * m * n, transcendentals=0),
        name="left_curve",
    )(side, *halves, far(right), far(f))


def right_curve_kernel(tile, flag_ref, a_ref, t_ref, b_ref, f_ref, i_ref, o_ref, q_ref):
    m = a_ref.shape[0]
    own = flag_ref[0, 0] > 0
    q = jnp.where(own, t_ref[...].astype(f32), b_ref[...].astype(f32))
    q_ref[...] = q.astype(bf16)

    @pl.when(pl.program_id(0) == 0)
    def _():
        o_ref[...] = i_ref[...]

    o_ref[1] += fold(q * q)

    def step_rows(i):
        rows = span(i, tile)
        image = jnp.dot(a_ref[rows, :], q_ref[...], preferred_element_type=f32)
        o_ref[0] += fold(f_ref[rows, :].astype(f32) * (image * image))
    each(m // tile, UNROLL, step_rows)


def right_curve(flag, left_new, total, back, f, sums, offset, width):
    m, rank = left_new.shape
    bn = pick(width, 2 * BLOCK, offset)
    base = offset // bn
    tall = pl.BlockSpec((rank, bn), lambda j: (0, j))
    small = pl.BlockSpec((2, 8, 128), lambda j: (0, 0, 0))
    return pl.pallas_call(
        functools.partial(right_curve_kernel, pick(m, TILE)),
        grid=(width // bn,),
        in_specs=[pl.BlockSpec(memory_space=pltpu.SMEM), pl.BlockSpec((m, rank), lambda j: (0, 0)), tall, tall,
                  pl.BlockSpec((m, bn), lambda j: (0, base + j)), small],
        out_specs=[small, tall],
        out_shape=[jax.ShapeDtypeStruct((2, 8, 128), f32), jax.ShapeDtypeStruct((rank, width), bf16)],
        compiler_params=pltpu.CompilerParams(vmem_limit_bytes=LIMIT),
        cost_estimate=pl.CostEstimate(flops=2 * m * width * rank, bytes_accessed=2 * m * width, transcendentals=0),
        name="right_curve",
    )(flag, left_new, total, back, far(f), sums)


def left_new_kernel(copies, *refs):
    l_ref, d_ref = refs[:2]
    step_ref, new_ref, t_ref, pair_ref = refs[-4:]
    rank = l_ref.shape[1]
    step = step_of(total_of(refs[2:-4]), copies)
    step_ref[...] = jnp.broadcast_to(step, (8, 128))
    left = l_ref[...].astype(f32)
    descent = d_ref[...]
    new = left + step * descent
    new_ref[...] = new.astype(bf16)
    t_ref[...] = new.T.astype(bf16)
    moved = left + step * descent.astype(bf16).astype(f32)
    high = moved.astype(bf16)
    pair_ref[:, :rank] = high
    pair_ref[:, rank:] = (moved - high.astype(f32)).astype(bf16)


def left_update(left, descent, pieces, copies):
    m, rank = left.shape
    return pl.pallas_call(
        functools.partial(left_new_kernel, copies),
        out_shape=[jax.ShapeDtypeStruct((8, 128), f32), pltpu.VMEM((m, rank), bf16), pltpu.VMEM((rank, m), bf16),
                   pltpu.VMEM((m, 2 * rank), bf16)],
        compiler_params=pltpu.CompilerParams(vmem_limit_bytes=LIMIT),
        cost_estimate=pl.CostEstimate(flops=2 * m * rank, bytes_accessed=10 * m * rank, transcendentals=0),
        name="left_update",
    )(left, near(descent), *pieces)


def partial_kernel(tile, p_ref, w_ref, r_ref, f_ref, t_ref, k_ref, o_ref, acc_ref):
    m = p_ref.shape[0]
    acc_ref[...] = jnp.zeros_like(acc_ref)

    def step_rows(i):
        rows = span(i, tile)
        image = lax.dot_general(p_ref[rows, :], r_ref[...], NT, preferred_element_type=f32)
        later = w_ref[rows, :].astype(f32) - image
        weighted = (f_ref[rows, :].astype(f32) * later).astype(bf16)
        acc_ref[...] += jnp.dot(t_ref[:, rows], weighted, preferred_element_type=f32)
    each(m // tile, UNROLL, step_rows)
    o_ref[...] = acc_ref[...].astype(o_ref.dtype)


def partial_pass(pair, w, twice, f, new_t, token, offset, width):
    m, n = w.shape
    rank = new_t.shape[0]
    bn = pick(width, WIDE, offset)
    base = offset // bn
    tile = pick(m, TILE)
    wide = pl.BlockSpec((m, bn), lambda j: (0, base + j))
    return pl.pallas_call(
        functools.partial(partial_kernel, tile),
        grid=(width // bn,),
        in_specs=[pl.BlockSpec((m, 2 * rank), lambda j: (0, 0)), wide,
                  pl.BlockSpec((bn, 2 * rank), lambda j: (base + j, 0)), wide,
                  pl.BlockSpec((rank, m), lambda j: (0, 0)), pl.BlockSpec(memory_space=pl.ANY)],
        out_specs=pl.BlockSpec((rank, bn), lambda j: (0, j)),
        out_shape=jax.ShapeDtypeStruct((rank, width), bf16),
        scratch_shapes=[pltpu.VMEM((rank, bn), f32)],
        compiler_params=pltpu.CompilerParams(vmem_limit_bytes=LIMIT),
        cost_estimate=pl.CostEstimate(flops=6 * m * width * rank, bytes_accessed=4 * m * width, transcendentals=0),
        name="partial_pass",
    )(near(pair), far(w), far(twice), far(f), near(new_t), token)


def last_kernel(tile, copies, edges, *refs):
    w_ref, p_ref, r_ref, n_ref = refs[:4]
    q_refs = refs[4:4 + len(edges)]
    pieces = refs[4 + len(edges):-3]
    o_ref, new_ref, q_ref = refs[-3:]
    j = pl.program_id(0)
    s2 = step_of(total_of(pieces), copies)
    m = p_ref.shape[0]
    rank = n_ref.shape[1]
    for (first, count), ref in zip(edges, q_refs):
        @pl.when((j >= first) & (j < first + count))
        def _():
            q_ref[...] = ref[...]

    def step_rows(i):
        rows = span(i, tile)
        image = lax.dot_general(p_ref[rows, :], r_ref[...], NT, preferred_element_type=f32)
        second = jnp.dot(n_ref[rows, :], q_ref[...], preferred_element_type=f32)
        later = w_ref[rows, :].astype(f32) - image
        o_ref[rows, :] = (later - s2 * second).astype(o_ref.dtype)
    each(m // tile, UNROLL, step_rows)
    new_ref[...] = (r_ref[:, :rank].astype(f32) + s2 * q_ref[...].astype(f32).T).astype(bf16)


def last_pass(w, pair, twice, left_new, parts, pieces, copies):
    m, n = w.shape
    rank = left_new.shape[1]
    common = n
    at = 0
    edges = []
    for part in parts:
        common = math.gcd(common, part.shape[1])
    bn = pick(common, 3 * BLOCK // 2)
    for part in parts:
        edges.append((at // bn, part.shape[1] // bn))
        at += part.shape[1]
    whole = pl.BlockSpec((m, rank), lambda j: (0, 0))
    wide = pl.BlockSpec((m, bn), lambda j: (0, j))
    side = pl.BlockSpec((bn, rank), lambda j: (j, 0))

    def tall(first, count):
        return pl.BlockSpec((rank, bn), lambda j: (0, jnp.clip(j - first, 0, count - 1)))

    return pl.pallas_call(
        functools.partial(last_kernel, pick(m, TILE), copies, tuple(edges)),
        grid=(n // bn,),
        in_specs=[wide, pl.BlockSpec((m, 2 * rank), lambda j: (0, 0)), pl.BlockSpec((bn, 2 * rank), lambda j: (j, 0)), whole]
        + [tall(*edge) for edge in edges]
        + [pl.BlockSpec((2, 8, 128), lambda j: (0, 0, 0))] * len(pieces),
        out_specs=[wide, side],
        out_shape=[jax.ShapeDtypeStruct((m, n), bf16), jax.ShapeDtypeStruct((n, rank), bf16)],
        scratch_shapes=[pltpu.VMEM((rank, bn), bf16)],
        compiler_params=pltpu.CompilerParams(vmem_limit_bytes=LIMIT),
        cost_estimate=pl.CostEstimate(flops=6 * m * n * rank, bytes_accessed=4 * m * n, transcendentals=0),
        name="last_pass",
    )(far(w), near(pair), far(twice), left_new, *parts, *pieces)


FIRST = (3, 2, 1)
SECOND = (1, 1, 1, 1)
ORDER = (
    ("p", 0), ("p", 1), ("p", 2), ("h", 0), ("p", 3), ("h", 1), ("t", 0), ("h", 2), ("t", 1),
    ("h", 3), ("v", 0), ("t", 2), ("v", 1), ("t", 3), ("v", 2), ("v", 3),
)


def cut(extent, weights):
    units = extent // 128 if extent % 128 == 0 else 1
    size = extent // units
    total = sum(weights)
    edges = [0]
    seen = 0
    for weight in weights:
        seen += weight
        edges.append(units * seen // total)
    return [(a * size, (b - a) * size) for a, b in zip(edges, edges[1:]) if b > a]


def other(count, bit):
    return [(i, i ^ bit) for i in range(count)]


def turned(count, by):
    return [(i, (i + by) % count) for i in range(count)]


def pieces_of(x, axis):
    if lax.axis_size(axis) == 4:
        return [x] + [lax.ppermute(x, axis, turned(4, k)) for k in (1, 2, 3)]
    return [add_up(x, axis)]


def add_up(x, axis):
    count = lax.axis_size(axis)
    if count == 4:
        own, one, two, three = pieces_of(x, axis)
        return (own + two) + (one + three)
    if count & (count - 1):
        return lax.psum(x, axis)
    bit = 1
    while bit < count:
        x = x + lax.ppermute(x, axis, other(count, bit))
        bit *= 2
    return x


def line_order(axis):
    at = lax.axis_index(axis)
    low = at < 2
    return [at, at ^ 1, jnp.where(low, 2, 1), jnp.where(low, 3, 0)]


def sum_columns(x, axis):
    count = lax.axis_size(axis)
    if count != 4 or x.shape[0] % 32:
        whole = lax.psum(x, axis)
        return whole[:x.shape[0] // 2], whole[x.shape[0] // 2:]
    side = lax.axis_index(axis) & 1
    half = x.shape[0] // 2
    mine = lax.dynamic_slice_in_dim(x, side * half, half, 0)
    theirs = lax.dynamic_slice_in_dim(x, (1 - side) * half, half, 0)
    chip = (mine + lax.ppermute(theirs, axis, other(4, 1))).astype(bf16)
    both = chip.astype(f32) + lax.ppermute(chip, axis, other(4, 2)).astype(f32)
    return both, lax.ppermute(both, axis, other(4, 1))


def after(x, *others):
    return lax.optimization_barrier((x,) + others)[0]


def right_sum(make, finish, chunks, axis):
    count = len(chunks)
    sent = [None] * count
    halves = [None] * count
    totals = [None] * count
    backs = [None] * count
    token = None

    def part(k):
        nonlocal token
        sent[k] = make(k, token)
        token = sent[k]

    def half(k):
        nonlocal token
        came = lax.ppermute(sent[k], axis, [(0, 1), (3, 2)])
        mine = after(sent[k], token)
        token = halves[k] = (mine.astype(f32) + came.astype(f32)).astype(mine.dtype)

    def total(k):
        nonlocal token
        across = lax.ppermute(halves[k], axis, [(1, 2), (2, 1)])
        mine = after(halves[k], token)
        token = totals[k] = (mine.astype(f32) + across.astype(f32)).astype(mine.dtype)

    def back(k):
        nonlocal token
        backs[k] = lax.ppermute(totals[k], axis, [(1, 0), (2, 3)])
        token = finish(k, totals[k], backs[k], token)

    for name, k in ORDER:
        (part, half, total, back)["phtv".index(name)](k)


def body(activations, out_grads, matrix, left, right):
    col_count = lax.axis_size("col")
    row_count = lax.axis_size("row")
    m, n = matrix.shape
    shard = out_grads.shape[0]
    line = row_count == 4 and col_count == 4
    twice = jnp.concatenate([right, right], axis=1)
    prev = None
    if line:
        outward = [(0, 1), (1, 0), (2, 3), (3, 2)]
        across = [(1, 2), (2, 1)]
        onward = [(1, 0), (2, 3)]
        outer = lax.ppermute(out_grads, "row", outward)
        inner = lax.ppermute(out_grads, "row", across)
        chunks = cut(n, FIRST)
        outers = [lax.slice_in_dim(outer, o, o + k, axis=1) for o, k in chunks]
        inners = [lax.slice_in_dim(inner, o, o + k, axis=1) for o, k in chunks]
        beside = lax.ppermute(activations, "col", other(4, 1))
        beyond = lax.ppermute(activations, "col", other(4, 2))
        crossed = [lax.ppermute(after(outers[0], beside, beyond), "row", across)]
        crossed += [lax.ppermute(after(x, crossed[0]), "row", across) for x in outers[1:]]
        corner = lax.ppermute(after(beyond, crossed[0]), "col", other(4, 1))
        blocks = jnp.stack([activations, beside, beyond, corner])
        me = lax.axis_index("col")
        ordered = jnp.concatenate([lax.dynamic_index_in_dim(blocks, k ^ me, 0, False) for k in line_order("row")], axis=0)
        at = ordered.T
        partials = []
        for k, (offset, width) in enumerate(chunks):
            if k == 0:
                early = lax.ppermute(inners[0], "row", onward)
                late = lax.ppermute(after(crossed[0], early), "row", onward)
                ends = [(early, shard, 0, False), (late, shard, 0, False)]
            else:
                both = jnp.concatenate([inners[k], crossed[k]], axis=0)
                both = after(both, at if k == 1 else partials[k - 2])
                end = lax.ppermute(both, "row", onward)
                ends = [(end, shard, 0, False), (end, shard, 1, False)]
            groups = [[(out_grads, shard, 0, True)], [(outer, shard, 0, True)],
                      [(inner, shard, 0, True), ends[0]], [(crossed[k], shard, 0, False), ends[1]]]
            prev = first_pass(at, matrix, left, right, groups, offset, width, prev, BLOCK, 2 * TILE)
            partials.append(prev[1])
    else:
        gathered = lax.all_gather(activations, "col", axis=0, tiled=True)
        grads = lax.all_gather(out_grads, "row", axis=0, tiled=True)
        prev = first_pass(gathered.T, matrix, left, right, [[(grads, grads.shape[0], 0, True)]], 0, n, None, BLOCK, TILE)
    fisher, partial = prev
    halves = sum_columns(partial, "col")
    side = lax.axis_index("col") & 1 if col_count == 4 else 0
    sums, left_descent = left_curve(jnp.full((1, 1), side, jnp.int32), halves, right, fisher)
    pieces = pieces_of(add_up(sums, "col"), "row")
    step, left_new, new_t, pair = left_update(left, left_descent, pieces, col_count)
    central = (lax.axis_index("row") % 3 != 0) if line else True
    flag = jnp.full((1, 1), central, jnp.int32)
    chunks = cut(n, SECOND)
    sums = jnp.zeros((2, 8, 128), f32)
    parts = [None] * len(chunks)

    def make(k, token):
        return partial_pass(pair, matrix, twice, fisher, new_t, step if token is None else token, *chunks[k])

    def finish(k, total, back, token):
        nonlocal sums
        if token is not None:
            total = after(total, token)
        sums, parts[k] = right_curve(flag, left_new, total, back, fisher, sums, *chunks[k])
        return sums

    if line:
        right_sum(make, finish, chunks, "row")
    else:
        for k in range(len(chunks)):
            total = lax.psum(make(k, None), "row")
            finish(k, total, total, None)
    pieces = pieces_of(add_up(sums, "col"), "row")
    residual, right_new = last_pass(matrix, pair, twice, left_new, parts, pieces, row_count)
    return (left_new, right_new, residual)


def solution(mesh):
    placed = (
        P(("grp", "col"), "row"),
        P(("grp", "row"), "col"),
        P(("grp", "row"), "col"),
        P(("grp", "row"), None),
        P(("grp", "col"), None),
    )
    return jax.shard_map(
        body,
        mesh=mesh,
        in_specs=placed,
        out_specs=(P(("grp", "row"), None), P(("grp", "col"), None), P(("grp", "row"), "col")),
        check_vma=False,
    )
```

```python
import functools
import math
import jax
import jax.numpy as jnp
from jax import lax
from jax.experimental import pallas as pl
from jax.experimental.pallas import tpu as pltpu
from jax.sharding import PartitionSpec as P

f32 = jnp.float32
bf16 = jnp.bfloat16
NT = (((1,), (1,)), ((), ()))
epsilon = 1e-06
BLOCK = 768
WIDE = 384
TILE = 768
MB = 1 << 20
LIMIT = 48 * MB


def near(x):
    return pltpu.with_memory_space_constraint(x, pltpu.VMEM)


def far(x):
    return pltpu.with_memory_space_constraint(x, pltpu.HBM)


def pick(extent, want, offset=0):
    for size in range(min(want, extent), 0, -1):
        if extent % size == 0 and offset % size == 0 and (size % 128 == 0 or size == extent):
            return size
    return extent


def each(count, unroll, step):
    if unroll:
        for i in range(count):
            step(i)
    else:
        pl.loop(0, count)(step)


def span(i, tile):
    return pl.ds(i * tile, tile) if isinstance(i, int) else pl.ds(pl.multiple_of(i * tile, tile), tile)


UNROLL = True


def fold(x):
    rows, cols = x.shape
    y = x.reshape(rows // 8, 8, cols).sum(axis=0)
    out = y[:, :128]
    for at in range(128, cols, 128):
        out = out + y[:, at:at + 128]
    return out


def first_kernel(groups, tile, has_prev, *refs):
    at_ref, w_ref, l_ref, r_ref = refs[:4]
    used = 4
    parts = []
    for count in groups:
        parts.append(refs[used:used + count])
        used += count
    if has_prev:
        acc_in = refs[used]
        used += 2
    f_ref, acc_ref, g_ref = refs[used:used + 3]
    step = pl.program_id(0)
    at = 0
    for part in parts:
        total = part[0][...]
        for more in part[1:]:
            total = total + more[...]
        g_ref[pl.ds(at, total.shape[0]), :] = total
        at += total.shape[0]

    @pl.when(step == 0)
    def _():
        if has_prev:
            acc_ref[...] = acc_in[...]
        else:
            acc_ref[...] = jnp.zeros_like(acc_ref)

    m = at_ref.shape[0]

    def step_rows(i):
        rows = span(i, tile)
        grad = jnp.dot(at_ref[rows, :], g_ref[...], preferred_element_type=f32)
        image = lax.dot_general(l_ref[rows, :], r_ref[...], NT, preferred_element_type=f32)
        w = w_ref[rows, :].astype(f32)
        x = w * grad
        fisher = 1.0 + x * x
        f_ref[rows, :] = fisher.astype(f_ref.dtype)
        weighted = (fisher * (w - image)).astype(bf16)
        acc_ref[rows, :] += jnp.dot(weighted, r_ref[...], preferred_element_type=f32)
    each(m // tile, UNROLL, step_rows)


def first_pass(at, w, left, right, groups, offset, width, prev, block=512, tile=512, fdt=bf16):
    m, n = w.shape
    rank = left.shape[1]
    tokens = at.shape[1]
    bn = pick(width, block, offset)
    tile = pick(m, tile)
    base = offset // bn
    flat = [p for g in groups for p in g]
    ins = [near(at), far(w), far(left), far(right)] + [far(p[0]) for p in flat]

    def piece(array, rows, row, whole):
        shift = base if whole else 0
        return pl.BlockSpec((rows, bn), lambda j: (row, shift + j))

    specs = [
        pl.BlockSpec((m, tokens), lambda j: (0, 0)),
        pl.BlockSpec((m, bn), lambda j: (0, base + j)),
        pl.BlockSpec((m, rank), lambda j: (0, 0)),
        pl.BlockSpec((bn, rank), lambda j: (base + j, 0)),
    ] + [piece(*p) for p in flat]
    alias = {}
    if prev is not None:
        fprev, accprev = prev
        alias = {len(ins): 1, len(ins) + 1: 0}
        ins += [near(accprev), far(fprev)]
        specs += [pl.BlockSpec((m, rank), lambda j: (0, 0)), pl.BlockSpec(memory_space=pl.ANY)]
    cost = pl.CostEstimate(flops=2 * m * width * (tokens + 2 * rank), bytes_accessed=m * width * 4, transcendentals=0)
    return pl.pallas_call(
        functools.partial(first_kernel, tuple(len(g) for g in groups), tile, prev is not None),
        grid=(width // bn,),
        in_specs=specs,
        out_specs=[pl.BlockSpec((m, bn), lambda j: (0, base + j)), pl.BlockSpec((m, rank), lambda j: (0, 0))],
        out_shape=[pltpu.HBM((m, n), fdt), pltpu.VMEM((m, rank), f32)],
        scratch_shapes=[pltpu.VMEM((tokens, bn), bf16)],
        input_output_aliases=alias,
        compiler_params=pltpu.CompilerParams(vmem_limit_bytes=LIMIT),
        cost_estimate=cost,
        name="first_pass",
    )(*ins)


def total_of(refs):
    if len(refs) == 4:
        return (refs[0][...] + refs[2][...]) + (refs[1][...] + refs[3][...])
    return refs[0][...]


def step_of(total, copies):
    curve = jnp.sum(total[0], axis=(0, 1), keepdims=True)
    norm = jnp.sum(total[1], axis=(0, 1), keepdims=True) * (1.0 / copies)
    return norm / (curve + epsilon)


def left_curve_kernel(tile, side_ref, b_ref, c_ref, r_ref, f_ref, o_ref, d_ref, a_ref):
    m = d_ref.shape[0]
    half = m // 2

    @pl.when(pl.program_id(0) == 0)
    def _():
        low = side_ref[0, 0] == 0
        total = jnp.zeros((8, 128), f32)
        for at, first, second in ((0, b_ref, c_ref), (half, c_ref, b_ref)):
            d = jnp.where(low, first[...], second[...])
            d_ref[pl.ds(at, half), :] = d
            a_ref[pl.ds(at, half), :] = d.astype(bf16)
            total = total + fold(d * d)
        o_ref[0] = jnp.zeros((8, 128), f32)
        o_ref[1] = total

    def step_rows(i):
        rows = span(i, tile)
        image = lax.dot_general(a_ref[rows, :], r_ref[...], NT, preferred_element_type=f32)
        o_ref[0] += fold(f_ref[rows, :].astype(f32) * (image * image))
    each(m // tile, UNROLL, step_rows)


def left_curve(side, halves, right, f):
    m, n = f.shape
    rank = right.shape[1]
    bn = pick(n, 3 * BLOCK)
    half = pl.BlockSpec((m // 2, rank), lambda j: (0, 0))
    return pl.pallas_call(
        functools.partial(left_curve_kernel, pick(m, TILE)),
        grid=(n // bn,),
        in_specs=[pl.BlockSpec(memory_space=pltpu.SMEM), half, half, pl.BlockSpec((bn, rank), lambda j: (j, 0)),
                  pl.BlockSpec((m, bn), lambda j: (0, j))],
        out_specs=[pl.BlockSpec((2, 8, 128), lambda j: (0, 0, 0)), pl.BlockSpec((m, rank), lambda j: (0, 0))],
        out_shape=[jax.ShapeDtypeStruct((2, 8, 128), f32), pltpu.VMEM((m, rank), f32)],
        scratch_shapes=[pltpu.VMEM((m, rank), bf16)],
        compiler_params=pltpu.CompilerParams(vmem_limit_bytes=LIMIT),
        cost_estimate=pl.CostEstimate(flops=2 * m * n * rank, bytes_accessed=2 * m * n, transcendentals=0),
        name="left_curve",
    )(side, *halves, far(right), far(f))


def right_curve_kernel(tile, flag_ref, a_ref, t_ref, b_ref, f_ref, i_ref, o_ref, q_ref):
    m = a_ref.shape[0]
    own = flag_ref[0, 0] > 0
    q = jnp.where(own, t_ref[...].astype(f32), b_ref[...].astype(f32))
    q_ref[...] = q.astype(bf16)

    @pl.when(pl.program_id(0) == 0)
    def _():
        o_ref[...] = i_ref[...]

    o_ref[1] += fold(q * q)

    def step_rows(i):
        rows = span(i, tile)
        image = jnp.dot(a_ref[rows, :], q_ref[...], preferred_element_type=f32)
        o_ref[0] += fold(f_ref[rows, :].astype(f32) * (image * image))
    each(m // tile, UNROLL, step_rows)


def right_curve(flag, left_new, total, back, f, sums, offset, width):
    m, rank = left_new.shape
    bn = pick(width, 2 * BLOCK, offset)
    base = offset // bn
    tall = pl.BlockSpec((rank, bn), lambda j: (0, j))
    small = pl.BlockSpec((2, 8, 128), lambda j: (0, 0, 0))
    return pl.pallas_call(
        functools.partial(right_curve_kernel, pick(m, TILE)),
        grid=(width // bn,),
        in_specs=[pl.BlockSpec(memory_space=pltpu.SMEM), pl.BlockSpec((m, rank), lambda j: (0, 0)), tall, tall,
                  pl.BlockSpec((m, bn), lambda j: (0, base + j)), small],
        out_specs=[small, tall],
        out_shape=[jax.ShapeDtypeStruct((2, 8, 128), f32), jax.ShapeDtypeStruct((rank, width), bf16)],
        compiler_params=pltpu.CompilerParams(vmem_limit_bytes=LIMIT),
        cost_estimate=pl.CostEstimate(flops=2 * m * width * rank, bytes_accessed=2 * m * width, transcendentals=0),
        name="right_curve",
    )(flag, left_new, total, back, far(f), sums)


def left_new_kernel(copies, *refs):
    l_ref, d_ref = refs[:2]
    step_ref, new_ref, t_ref, pair_ref = refs[-4:]
    rank = l_ref.shape[1]
    step = step_of(total_of(refs[2:-4]), copies)
    step_ref[...] = jnp.broadcast_to(step, (8, 128))
    left = l_ref[...].astype(f32)
    descent = d_ref[...]
    new = left + step * descent
    new_ref[...] = new.astype(bf16)
    t_ref[...] = new.T.astype(bf16)
    moved = left + step * descent.astype(bf16).astype(f32)
    high = moved.astype(bf16)
    pair_ref[:, :rank] = high
    pair_ref[:, rank:] = (moved - high.astype(f32)).astype(bf16)


def left_update(left, descent, pieces, copies):
    m, rank = left.shape
    return pl.pallas_call(
        functools.partial(left_new_kernel, copies),
        out_shape=[jax.ShapeDtypeStruct((8, 128), f32), pltpu.VMEM((m, rank), bf16), pltpu.VMEM((rank, m), bf16),
                   pltpu.VMEM((m, 2 * rank), bf16)],
        compiler_params=pltpu.CompilerParams(vmem_limit_bytes=LIMIT),
        cost_estimate=pl.CostEstimate(flops=2 * m * rank, bytes_accessed=10 * m * rank, transcendentals=0),
        name="left_update",
    )(left, near(descent), *pieces)


def moved_image(p_ref, rows, r_ref):
    rank = r_ref.shape[1]
    high = lax.dot_general(p_ref[rows, :rank], r_ref[...], NT, preferred_element_type=f32)
    return high + lax.dot_general(p_ref[rows, rank:], r_ref[...], NT, preferred_element_type=f32)


def partial_kernel(tile, p_ref, w_ref, r_ref, f_ref, t_ref, k_ref, o_ref, acc_ref):
    m = p_ref.shape[0]
    acc_ref[...] = jnp.zeros_like(acc_ref)

    def step_rows(i):
        rows = span(i, tile)
        image = moved_image(p_ref, rows, r_ref)
        later = w_ref[rows, :].astype(f32) - image
        weighted = (f_ref[rows, :].astype(f32) * later).astype(bf16)
        acc_ref[...] += jnp.dot(t_ref[:, rows], weighted, preferred_element_type=f32)
    each(m // tile, UNROLL, step_rows)
    o_ref[...] = acc_ref[...].astype(o_ref.dtype)


def partial_pass(pair, w, right, f, new_t, token, offset, width):
    m, n = w.shape
    rank = new_t.shape[0]
    bn = pick(width, WIDE, offset)
    base = offset // bn
    tile = pick(m, TILE)
    wide = pl.BlockSpec((m, bn), lambda j: (0, base + j))
    return pl.pallas_call(
        functools.partial(partial_kernel, tile),
        grid=(width // bn,),
        in_specs=[pl.BlockSpec((m, 2 * rank), lambda j: (0, 0)), wide,
                  pl.BlockSpec((bn, rank), lambda j: (base + j, 0)), wide,
                  pl.BlockSpec((rank, m), lambda j: (0, 0)), pl.BlockSpec(memory_space=pl.ANY)],
        out_specs=pl.BlockSpec((rank, bn), lambda j: (0, j)),
        out_shape=jax.ShapeDtypeStruct((rank, width), bf16),
        scratch_shapes=[pltpu.VMEM((rank, bn), f32)],
        compiler_params=pltpu.CompilerParams(vmem_limit_bytes=LIMIT),
        cost_estimate=pl.CostEstimate(flops=6 * m * width * rank, bytes_accessed=4 * m * width, transcendentals=0),
        name="partial_pass",
    )(near(pair), far(w), far(right), far(f), near(new_t), token)


def last_kernel(tile, copies, edges, *refs):
    w_ref, p_ref, r_ref, n_ref = refs[:4]
    q_refs = refs[4:4 + len(edges)]
    pieces = refs[4 + len(edges):-3]
    o_ref, new_ref, q_ref = refs[-3:]
    j = pl.program_id(0)
    s2 = step_of(total_of(pieces), copies)
    m = p_ref.shape[0]
    for (first, count), ref in zip(edges, q_refs):
        @pl.when((j >= first) & (j < first + count))
        def _():
            q_ref[...] = ref[...]

    def step_rows(i):
        rows = span(i, tile)
        image = moved_image(p_ref, rows, r_ref)
        second = jnp.dot(n_ref[rows, :], q_ref[...], preferred_element_type=f32)
        later = w_ref[rows, :].astype(f32) - image
        o_ref[rows, :] = (later - s2 * second).astype(o_ref.dtype)
    each(m // tile, UNROLL, step_rows)
    new_ref[...] = (r_ref[...].astype(f32) + s2 * q_ref[...].astype(f32).T).astype(bf16)


def last_pass(w, pair, right, left_new, parts, pieces, copies):
    m, n = w.shape
    rank = left_new.shape[1]
    common = n
    at = 0
    edges = []
    for part in parts:
        common = math.gcd(common, part.shape[1])
    bn = pick(common, 3 * BLOCK // 2)
    for part in parts:
        edges.append((at // bn, part.shape[1] // bn))
        at += part.shape[1]
    whole = pl.BlockSpec((m, rank), lambda j: (0, 0))
    wide = pl.BlockSpec((m, bn), lambda j: (0, j))
    side = pl.BlockSpec((bn, rank), lambda j: (j, 0))

    def tall(first, count):
        return pl.BlockSpec((rank, bn), lambda j: (0, jnp.clip(j - first, 0, count - 1)))

    return pl.pallas_call(
        functools.partial(last_kernel, pick(m, TILE), copies, tuple(edges)),
        grid=(n // bn,),
        in_specs=[wide, pl.BlockSpec((m, 2 * rank), lambda j: (0, 0)), pl.BlockSpec((bn, rank), lambda j: (j, 0)), whole]
        + [tall(*edge) for edge in edges]
        + [pl.BlockSpec((2, 8, 128), lambda j: (0, 0, 0))] * len(pieces),
        out_specs=[wide, side],
        out_shape=[jax.ShapeDtypeStruct((m, n), bf16), jax.ShapeDtypeStruct((n, rank), bf16)],
        scratch_shapes=[pltpu.VMEM((rank, bn), bf16)],
        compiler_params=pltpu.CompilerParams(vmem_limit_bytes=LIMIT),
        cost_estimate=pl.CostEstimate(flops=6 * m * n * rank, bytes_accessed=4 * m * n, transcendentals=0),
        name="last_pass",
    )(far(w), near(pair), far(right), left_new, *parts, *pieces)


FIRST = (3, 2, 1)
SECOND = (1, 1, 1, 1)
ORDER = (
    ("p", 0), ("p", 1), ("p", 2), ("h", 0), ("p", 3), ("h", 1), ("t", 0), ("h", 2), ("t", 1),
    ("h", 3), ("v", 0), ("t", 2), ("v", 1), ("t", 3), ("v", 2), ("v", 3),
)


def cut(extent, weights):
    units = extent // 128 if extent % 128 == 0 else 1
    size = extent // units
    total = sum(weights)
    edges = [0]
    seen = 0
    for weight in weights:
        seen += weight
        edges.append(units * seen // total)
    return [(a * size, (b - a) * size) for a, b in zip(edges, edges[1:]) if b > a]


def other(count, bit):
    return [(i, i ^ bit) for i in range(count)]


def turned(count, by):
    return [(i, (i + by) % count) for i in range(count)]


def pieces_of(x, axis):
    if lax.axis_size(axis) == 4:
        return [x] + [lax.ppermute(x, axis, turned(4, k)) for k in (1, 2, 3)]
    return [add_up(x, axis)]


def add_up(x, axis):
    count = lax.axis_size(axis)
    if count == 4:
        own, one, two, three = pieces_of(x, axis)
        return (own + two) + (one + three)
    if count & (count - 1):
        return lax.psum(x, axis)
    bit = 1
    while bit < count:
        x = x + lax.ppermute(x, axis, other(count, bit))
        bit *= 2
    return x


def line_order(axis):
    at = lax.axis_index(axis)
    low = at < 2
    return [at, at ^ 1, jnp.where(low, 2, 1), jnp.where(low, 3, 0)]


def sum_columns(x, axis):
    count = lax.axis_size(axis)
    if count != 4 or x.shape[0] % 32:
        whole = lax.psum(x, axis)
        return whole[:x.shape[0] // 2], whole[x.shape[0] // 2:]
    side = lax.axis_index(axis) & 1
    half = x.shape[0] // 2
    mine = lax.dynamic_slice_in_dim(x, side * half, half, 0)
    theirs = lax.dynamic_slice_in_dim(x, (1 - side) * half, half, 0)
    chip = (mine + lax.ppermute(theirs, axis, other(4, 1))).astype(bf16)
    both = chip.astype(f32) + lax.ppermute(chip, axis, other(4, 2)).astype(f32)
    return both, lax.ppermute(both, axis, other(4, 1))


def after(x, *others):
    return lax.optimization_barrier((x,) + others)[0]


def right_sum(make, finish, chunks, axis):
    count = len(chunks)
    sent = [None] * count
    halves = [None] * count
    totals = [None] * count
    backs = [None] * count
    token = None

    def part(k):
        nonlocal token
        sent[k] = make(k, token)
        token = sent[k]

    def half(k):
        nonlocal token
        came = lax.ppermute(sent[k], axis, [(0, 1), (3, 2)])
        mine = after(sent[k], token)
        token = halves[k] = (mine.astype(f32) + came.astype(f32)).astype(mine.dtype)

    def total(k):
        nonlocal token
        across = lax.ppermute(halves[k], axis, [(1, 2), (2, 1)])
        mine = after(halves[k], token)
        token = totals[k] = (mine.astype(f32) + across.astype(f32)).astype(mine.dtype)

    def back(k):
        nonlocal token
        backs[k] = lax.ppermute(totals[k], axis, [(1, 0), (2, 3)])
        token = finish(k, totals[k], backs[k], token)

    for name, k in ORDER:
        (part, half, total, back)["phtv".index(name)](k)


def body(activations, out_grads, matrix, left, right):
    col_count = lax.axis_size("col")
    row_count = lax.axis_size("row")
    m, n = matrix.shape
    shard = out_grads.shape[0]
    line = row_count == 4 and col_count == 4
    prev = None
    if line:
        outward = [(0, 1), (1, 0), (2, 3), (3, 2)]
        across = [(1, 2), (2, 1)]
        onward = [(1, 0), (2, 3)]
        outer = lax.ppermute(out_grads, "row", outward)
        inner = lax.ppermute(out_grads, "row", across)
        chunks = cut(n, FIRST)
        outers = [lax.slice_in_dim(outer, o, o + k, axis=1) for o, k in chunks]
        inners = [lax.slice_in_dim(inner, o, o + k, axis=1) for o, k in chunks]
        beside = lax.ppermute(activations, "col", other(4, 1))
        beyond = lax.ppermute(activations, "col", other(4, 2))
        crossed = [lax.ppermute(after(outers[0], beside, beyond), "row", across)]
        crossed += [lax.ppermute(after(x, crossed[0]), "row", across) for x in outers[1:]]
        corner = lax.ppermute(after(beyond, crossed[0]), "col", other(4, 1))
        blocks = jnp.stack([activations, beside, beyond, corner])
        me = lax.axis_index("col")
        ordered = jnp.concatenate([lax.dynamic_index_in_dim(blocks, k ^ me, 0, False) for k in line_order("row")], axis=0)
        at = ordered.T
        partials = []
        for k, (offset, width) in enumerate(chunks):
            if k == 0:
                early = lax.ppermute(inners[0], "row", onward)
                late = lax.ppermute(after(crossed[0], early), "row", onward)
                ends = [(early, shard, 0, False), (late, shard, 0, False)]
            else:
                both = jnp.concatenate([inners[k], crossed[k]], axis=0)
                both = after(both, at if k == 1 else partials[k - 2])
                end = lax.ppermute(both, "row", onward)
                ends = [(end, shard, 0, False), (end, shard, 1, False)]
            groups = [[(out_grads, shard, 0, True)], [(outer, shard, 0, True)],
                      [(inner, shard, 0, True), ends[0]], [(crossed[k], shard, 0, False), ends[1]]]
            prev = first_pass(at, matrix, left, right, groups, offset, width, prev, BLOCK, 2 * TILE)
            partials.append(prev[1])
    else:
        gathered = lax.all_gather(activations, "col", axis=0, tiled=True)
        grads = lax.all_gather(out_grads, "row", axis=0, tiled=True)
        prev = first_pass(gathered.T, matrix, left, right, [[(grads, grads.shape[0], 0, True)]], 0, n, None, BLOCK, TILE)
    fisher, partial = prev
    halves = sum_columns(partial, "col")
    side = lax.axis_index("col") & 1 if col_count == 4 else 0
    sums, left_descent = left_curve(jnp.full((1, 1), side, jnp.int32), halves, right, fisher)
    pieces = pieces_of(add_up(sums, "col"), "row")
    step, left_new, new_t, pair = left_update(left, left_descent, pieces, col_count)
    central = (lax.axis_index("row") % 3 != 0) if line else True
    flag = jnp.full((1, 1), central, jnp.int32)
    chunks = cut(n, SECOND)
    sums = jnp.zeros((2, 8, 128), f32)
    parts = [None] * len(chunks)

    def make(k, token):
        return partial_pass(pair, matrix, right, fisher, new_t, step if token is None else token, *chunks[k])

    def finish(k, total, back, token):
        nonlocal sums
        if token is not None:
            total = after(total, token)
        sums, parts[k] = right_curve(flag, left_new, total, back, fisher, sums, *chunks[k])
        return sums

    if line:
        right_sum(make, finish, chunks, "row")
    else:
        for k in range(len(chunks)):
            total = lax.psum(make(k, None), "row")
            finish(k, total, total, None)
    pieces = pieces_of(add_up(sums, "col"), "row")
    residual, right_new = last_pass(matrix, pair, right, left_new, parts, pieces, row_count)
    return (left_new, right_new, residual)


def solution(mesh):
    placed = (
        P(("grp", "col"), "row"),
        P(("grp", "row"), "col"),
        P(("grp", "row"), "col"),
        P(("grp", "row"), None),
        P(("grp", "col"), None),
    )
    return jax.shard_map(
        body,
        mesh=mesh,
        in_specs=placed,
        out_specs=(P(("grp", "row"), None), P(("grp", "col"), None), P(("grp", "row"), "col")),
        check_vma=False,
    )
```
